32 devices in a mesh: sec: 2 (over core), horiz: 4 (over z), lev: 4 (over y, x).
Axes of the slice: x: 2, y: 2, z: 4, core: 2. Of those that a mesh axis runs over, the one named last changes fastest.
Arguments:
- state: float32 [2, 80, 384, 128], P('sec', 'lev', 'horiz'), may hold values from -6 to 6
- diffusivity: float32 [2, 384, 128], P('sec', 'horiz'), may hold values from 0.02 to 0.24
- coupling_mask: int32 [2, 384, 128], P('sec', ('horiz', 'lev')), may hold values 0 or 1
- pair_rows: int32 [2, 384, 3], P('sec', ('horiz', 'lev')), may hold values from 0 to 383, as said below
- pair_counts: int32 [2, 384], P('sec', ('horiz', 'lev')), may hold values from 1 to 3
- remap_weights: bfloat16 [2, 384, 3, 128, 128], P('sec', ('horiz', 'lev')), may hold values from -0.3125 to 0.3125
- export_profile: float32 [2, 80], P('sec'), may hold values from 0.02 to 0.3
- import_profile: float32 [2, 80], P('sec'), may hold values from 0.1 to 1
- column_inverse: float32 [2, 80, 80], P('sec'), may hold values from -1 to 2
Outputs:
- new_state: float32 [2, 80, 384, 128], P('sec', 'lev', 'horiz')
- forcing: float32 [2, 384, 128], P('sec', ('horiz', 'lev'))
The draws below stay inside these ranges and needn't reach their ends.
Inputs may be any that keep to these rules, and one draw needn't show every extreme that they name: `pair_rows`: rows are grouped in aligned blocks of 24; for a row whose block starts at b, each entry p satisfies (p - b + 8) mod 384 < 40. Entries at positions of at least the row's count are padding.
All inputs are finite; a program needn't handle non-finite values. No bound on the sum of `coupling_mask` on one device may be relied on, other than what follows from the above.
Results may differ from the reference program's by a relative error of at most 0.0029.
Values may be sent and summed in bfloat16 or wider, within the bound.
A program may use at most 64 MiB of HBM per device.

```python
import math
import jax
import jax.numpy as jnp
from jax import lax

LEV = 80
W = 128
ROWS_DEV = 96
PAIRS = 3
REACH = 8
ATM_STEPS = 4
OCN_STEPS = 2
NR = 384
BLOCK_ROWS = 24
N_HORIZ = 4


def draw_pair_rows(key, part):
    key = jax.random.fold_in(key, 11)
    rows = jnp.arange(NR, dtype=jnp.int32)
    start = rows // BLOCK_ROWS * BLOCK_ROWS
    offset = jax.random.randint(key, (2, NR, PAIRS), 0, BLOCK_ROWS + 2 * REACH, dtype=jnp.int32)
    lowest = rows % BLOCK_ROWS == 0
    highest = rows % BLOCK_ROWS == BLOCK_ROWS - 1
    first_pair = jnp.arange(PAIRS, dtype=jnp.int32) == 0
    offset = jnp.where(lowest[None, :, None] & first_pair[None, None, :], 0, offset)
    offset = jnp.where(highest[None, :, None] & first_pair[None, None, :], BLOCK_ROWS + 2 * REACH - 1, offset)
    return jnp.mod(start[None, :, None] - REACH + offset, NR).astype(jnp.int32)


def draw_pair_counts(key, part):
    key = jax.random.fold_in(key, 12)
    rows = jnp.arange(NR, dtype=jnp.int32)
    counts = jax.random.randint(key, (2, NR), 1, PAIRS + 1, dtype=jnp.int32)
    lowest = rows % BLOCK_ROWS == 0
    return jnp.where(lowest[None, :], PAIRS, counts).astype(jnp.int32)


def draw_column_inverse(key, part):
    key = jax.random.fold_in(key, 13)
    noise = jnp.clip(jax.random.normal(key, (2, LEV, LEV), jnp.float32), -4.0, 4.0)
    rows = lax_iota_rows()
    return (rows + 0.35 * noise / math.sqrt(LEV)).astype(jnp.float32)


def lax_iota_rows():
    first = jnp.arange(LEV, dtype=jnp.int32)[:, None]
    second = jnp.arange(LEV, dtype=jnp.int32)[None, :]
    return jnp.where(first == second, 1.0, 0.0).astype(jnp.float32)[None]


def place_ends(values, rng, least, top_value):
    place = [jax.random.randint(jax.random.fold_in(rng, axis), (), 0, length) for axis, length in enumerate(values.shape)]
    main_axis = values.shape.index(max(values.shape))
    next_to = place[:main_axis] + [(place[main_axis] + 1) % values.shape[main_axis]] + place[main_axis + 1:]
    return values.at[tuple(place)].set(least).at[tuple(next_to)].set(top_value)


def block_scale(own_key, extent, cuts, least, high):
    def one(dim, blocks):
        steps = jax.random.uniform(jax.random.fold_in(jax.random.fold_in(own_key, 6), dim), (blocks,), jnp.float32, least / len(cuts), high / len(cuts))
        return jnp.repeat(jnp.exp(steps), extent[dim] // blocks).reshape((-1,) + (1,) * (len(extent) - dim - 1))

    loudness = one(*cuts[0])
    for cut in cuts[1:]:
        loudness = loudness * one(*cut)
    return loudness


def scatter_about(key, extent, width, limit, shards=(), kind=jnp.bfloat16):
    factor_of = block_scale(key, extent, shards, -0.22, 0.18) if shards else 1.0
    result = jax.random.normal(key, extent, jnp.float32) * width * factor_of
    return jnp.minimum(jnp.maximum(result, -limit), limit).astype(kind)


def setup_inputs(seed: int = 0) -> dict:
    arg_keys = jax.random.split(jax.random.key(seed), 10)
    state = scatter_about(arg_keys[0], (2, LEV, NR, W), 1.0, 6.0, ((0, 2), (1, 4), (2, 4)), jnp.float32)
    diffusivity = jnp.clip(jnp.exp(math.log(0.24) - 2.4849066 * jax.random.uniform(arg_keys[1], (2, NR, W), jnp.float32) ** block_scale(arg_keys[1], (2, NR, W), ((0, 2), (1, 4)), -0.2, 0.2)), 0.02, 0.24)
    coupling_mask = place_ends((jax.random.randint(arg_keys[2], (2, NR, W), 0, 4) < 3).astype(jnp.int32), jax.random.fold_in(arg_keys[2], 1), 0, 1)
    pair_rows = draw_pair_rows(jax.random.fold_in(arg_keys[9], 71), 0)
    pair_counts = draw_pair_counts(jax.random.fold_in(arg_keys[9], 71), 0)
    remap_weights = scatter_about(arg_keys[5], (2, NR, PAIRS, W, W), (W * PAIRS) ** -0.5, 0.3125, ((0, 2), (1, 16)))
    export_profile = jnp.clip(jnp.exp(math.log(0.3) - 2.7080503 * jax.random.uniform(arg_keys[6], (2, LEV), jnp.float32) ** block_scale(arg_keys[6], (2, LEV), ((0, 2),), -0.2, 0.2)), 0.02, 0.3)
    import_profile = jnp.clip(jnp.exp(math.log(1.0) - 2.3025851 * jax.random.uniform(arg_keys[7], (2, LEV), jnp.float32) ** block_scale(arg_keys[7], (2, LEV), ((0, 2),), -0.2, 0.2)), 0.1, 1.0)
    column_inverse = draw_column_inverse(jax.random.fold_in(arg_keys[9], 71), 0)
    return dict(state=state, diffusivity=diffusivity, coupling_mask=coupling_mask, pair_rows=pair_rows, pair_counts=pair_counts, remap_weights=remap_weights, export_profile=export_profile, import_profile=import_profile, column_inverse=column_inverse)


def substep(current, kappa):
    stencil = jnp.roll(current, 1, 1) + jnp.roll(current, -1, 1)
    stencil = stencil + jnp.roll(current, 1, 2) + jnp.roll(current, -1, 2) - 4.0 * current
    return current + kappa[None] * stencil


def regrid_section(partner, pair_rows, pair_counts, remap_weights):
    row_ids = pair_rows.reshape(N_HORIZ, ROWS_DEV, PAIRS)
    row_counts = pair_counts.reshape(N_HORIZ, ROWS_DEV)
    blocks = remap_weights.reshape(N_HORIZ, ROWS_DEV, PAIRS, W, W)

    def one_block(pieces):
        source_rows, counts_here, weights_here = pieces
        sources = partner[source_rows]
        usable = jnp.arange(PAIRS, dtype=jnp.int32)[None, :] < counts_here[:, None]
        sources = jnp.where(usable[:, :, None], sources, jnp.zeros((), sources.dtype))
        return jnp.einsum("rkw,rkwv->rv", sources.astype(jnp.float32), weights_here.astype(jnp.float32))

    return lax.map(one_block, (row_ids, row_counts, blocks)).reshape(NR, W)


def reference(state, diffusivity, coupling_mask, pair_rows, pair_counts, remap_weights, export_profile, import_profile, column_inverse):
    dynamic = []
    exports = []
    for section in range(2):
        current = state[section]
        count_steps = ATM_STEPS if section == 0 else OCN_STEPS
        for step_index in range(count_steps):
            current = substep(current, diffusivity[section])
        dynamic.append(current)
        surface_out = jnp.tensordot(export_profile[section], current, axes=(0, 0), precision=lax.Precision.HIGHEST)
        exports.append(surface_out.astype(jnp.bfloat16))
    results = []
    forcings = []
    for section in range(2):
        forcing = regrid_section(exports[1 - section], pair_rows[section], pair_counts[section], remap_weights[section])
        forcings.append(forcing)
        masked = forcing * coupling_mask[section].astype(jnp.float32)
        forced = dynamic[section] + import_profile[section][:, None, None] * masked[None]
        mixed_columns = jnp.tensordot(column_inverse[section], forced, axes=(1, 0), precision=lax.Precision.HIGHEST)
        results.append(mixed_columns)
    return jnp.stack(results), jnp.stack(forcings)
```

```python
import functools

import jax
import jax.numpy as jnp
from jax import lax
from jax.experimental import pallas as pl
from jax.experimental.pallas import tpu as pltpu
from jax.sharding import PartitionSpec as P

REACH = 8
ATM_STEPS = 4
OCN_STEPS = 2
HALO = 8
MARGIN = REACH + HALO
F32 = jnp.float32
BF16 = jnp.bfloat16


def diffuse(v, kappas):
    rows = v.shape[0]
    for k in kappas:
        around = (
            pltpu.roll(v, 1, 0)
            + pltpu.roll(v, rows - 1, 0)
            + pltpu.roll(v, 1, 1)
            + pltpu.roll(v, v.shape[1] - 1, 1)
        )
        v = v + k * (around - 4.0 * v)
    return v


def kernel(
    sizes,
    x_ref,
    kap_ref,
    mask_ref,
    rows_ref,
    counts_ref,
    w_hbm,
    exp_ref,
    imp_ref,
    inv_ref,
    out_ref,
    f_ref,
    w_buf,
    p_buf,
    part,
    kapw,
    halo_x,
    halo_k,
    dyn16,
    col16,
    c_buf,
    z_buf,
    y16,
    yr,
    fm,
    cs,
    w_sem,
    halo_s,
    halo_r,
    halok_s,
    halok_r,
    part_s,
    part_r,
    pedge_s,
    pedge_r,
    kapw_s,
    kapw_r,
    kedge_s,
    kedge_r,
    bulk_s,
    bulk_r,
    fm_s,
    fm_r,
    ret_s,
    ret_r,
):
    H, L, K, R, W = sizes
    B = R // L
    T = B // 8
    G = K // 2
    WIN = B + 2 * MARGIN
    LEV = K * L
    s = lax.axis_index("sec")
    h = lax.axis_index("horiz")
    l = lax.axis_index("lev")
    other = 1 - s
    nxt = lax.rem(h + 1, H)
    prv = lax.rem(h + H - 1, H)

    def remote(src, dst, ssem, rsem, dev):
        return pltpu.make_async_remote_copy(
            src_ref=src,
            dst_ref=dst,
            send_sem=ssem,
            recv_sem=rsem,
            device_id=dev,
            device_id_type=pl.DeviceIdType.MESH,
        )

    w_copy = pltpu.make_async_copy(w_hbm, w_buf, w_sem)
    w_copy.start()

    barrier = pltpu.get_barrier_semaphore()

    def greet(dev):
        pl.semaphore_signal(barrier, inc=1, device_id=dev, device_id_type=pl.DeviceIdType.MESH)

    for d in range(1, L):
        greet((s, h, lax.rem(l + d, L)))
    greet((s, nxt, l))
    greet((s, prv, l))
    for q in range(L):
        greet((other, h, q))

    @pl.when(l == 0)
    def _():
        for q in range(L):
            greet((other, prv, q))

    @pl.when(l == L - 1)
    def _():
        for q in range(L):
            greet((other, nxt, q))

    def add_level(k, acc):
        return acc + exp_ref[0, l * K + k] * x_ref[k]

    p_buf[...] = lax.fori_loop(0, K, add_level, jnp.zeros((R, W), F32), unroll=4)

    pl.semaphore_wait(barrier, (L - 1) + 2 + L + 2)

    halos = [
        remote(x_ref.at[:, pl.ds(R - HALO, HALO)], halo_x.at[0], halo_s.at[0], halo_r.at[0], (s, nxt, l)),
        remote(x_ref.at[:, pl.ds(0, HALO)], halo_x.at[1], halo_s.at[1], halo_r.at[1], (s, prv, l)),
        remote(kap_ref.at[pl.ds(R - HALO, HALO)], halo_k.at[0], halok_s.at[0], halok_r.at[0], (s, nxt, l)),
        remote(kap_ref.at[pl.ds(0, HALO)], halo_k.at[1], halok_s.at[1], halok_r.at[1], (s, prv, l)),
    ]
    for c in halos:
        c.start()

    def window(q):
        lo = max(q * B - MARGIN, 0)
        hi = min(q * B + B + MARGIN, R)
        return lo, lo - (q * B - MARGIN), hi - lo

    def part_copy(q):
        lo, at, n = window(q)
        return remote(
            p_buf.at[pl.ds(lo, n)], part.at[l, pl.ds(at, n)], part_s.at[q], part_r.at[l], (other, h, q)
        )

    def kap_copy(q):
        lo, at, n = window(q)
        return remote(kap_ref.at[pl.ds(lo, n)], kapw.at[pl.ds(at, n)], kapw_s, kapw_r, (other, h, q))

    edge_low = remote(
        p_buf.at[pl.ds(R - MARGIN, MARGIN)],
        part.at[l, pl.ds(0, MARGIN)],
        pedge_s.at[0],
        pedge_r.at[l],
        (other, nxt, 0),
    )
    edge_high = remote(
        p_buf.at[pl.ds(0, MARGIN)],
        part.at[l, pl.ds(WIN - MARGIN, MARGIN)],
        pedge_s.at[1],
        pedge_r.at[l],
        (other, prv, L - 1),
    )
    kedge_low = remote(
        kap_ref.at[pl.ds(R - MARGIN, MARGIN)], kapw.at[pl.ds(0, MARGIN)], kedge_s, kedge_r, (other, nxt, 0)
    )
    kedge_high = remote(
        kap_ref.at[pl.ds(0, MARGIN)],
        kapw.at[pl.ds(WIN - MARGIN, MARGIN)],
        kedge_s,
        kedge_r,
        (other, prv, L - 1),
    )
    for q in range(L):
        part_copy(q).start()
    edge_low.start()
    edge_high.start()
    for q in range(L):

        @pl.when(l == q)
        def _(q=q):
            kap_copy(q).start()

    @pl.when(l == 0)
    def _():
        kedge_low.start()

    @pl.when(l == L - 1)
    def _():
        kedge_high.start()

    steps = jnp.where(s == 0, ATM_STEPS, OCN_STEPS)
    steps_other = jnp.where(s == 0, OCN_STEPS, ATM_STEPS)

    def staged(k, count):
        return [k if i < OCN_STEPS else jnp.where(i < count, k, 0.0) for i in range(ATM_STEPS)]

    def keep(v, at, first, g, levels):
        for q, row in levels:
            for t in range(T):
                lo = row + 8 * t - first + at
                dyn16[q, t, g] = jnp.concatenate([v[0][lo : lo + 8], v[1][lo : lo + 8]], axis=0).astype(BF16)

    def bulk_copy(q, dst_slot):
        return remote(dyn16.at[q], col16.at[dst_slot], bulk_s.at[q], bulk_r.at[dst_slot], (s, h, q))

    def send_bulk(q):
        @pl.when(l != q)
        def _():
            bulk_copy(q, l).start()

        @pl.when(l == q)
        def _():
            col16[q] = dyn16[q]

    lo_c, hi_c = B - HALO, R - B + HALO
    k_mid = staged(kap_ref[lo_c:hi_c], steps)

    def middle(g, _):
        v = [diffuse(x_ref[2 * g + e, lo_c:hi_c, :], k_mid) for e in range(2)]
        for e in range(2):
            out_ref[2 * g + e, B : R - B, :] = v[e][HALO : HALO + R - 2 * B]
        keep(v, 0, lo_c, g, [(q, q * B) for q in range(1, L - 1)])
        return 0

    lax.fori_loop(0, G, middle, 0)
    for q in range(1, L - 1):
        send_bulk(q)

    for c in halos:
        c.wait_recv()

    k_top = staged(jnp.concatenate([halo_k[0], kap_ref[0 : B + HALO]], axis=0), steps)

    def top(g, _):
        v = [
            diffuse(jnp.concatenate([halo_x[0, 2 * g + e], x_ref[2 * g + e, 0 : B + HALO, :]], axis=0), k_top)
            for e in range(2)
        ]
        for e in range(2):
            out_ref[2 * g + e, 0:B, :] = v[e][HALO : HALO + B]
        keep(v, HALO, 0, g, [(0, 0)])
        return 0

    lax.fori_loop(0, G, top, 0)
    send_bulk(0)

    k_bot = staged(jnp.concatenate([kap_ref[R - B - HALO : R], halo_k[1]], axis=0), steps)

    def bottom(g, _):
        v = [
            diffuse(
                jnp.concatenate([x_ref[2 * g + e, R - B - HALO : R, :], halo_x[1, 2 * g + e]], axis=0), k_bot
            )
            for e in range(2)
        ]
        for e in range(2):
            out_ref[2 * g + e, R - B : R, :] = v[e][HALO : HALO + B]
        keep(v, HALO, R - B, g, [(L - 1, R - B)])
        return 0

    lax.fori_loop(0, G, bottom, 0)
    send_bulk(L - 1)

    inv = inv_ref[...]
    first = lax.broadcasted_iota(jnp.int32, (LEV, LEV), 0)
    second = lax.broadcasted_iota(jnp.int32, (LEV, LEV), 1)
    mix = inv - jnp.where(first == second, 1.0, 0.0)
    mix_hi = mix.astype(BF16)
    mix_lo = (mix - mix_hi.astype(F32)).astype(BF16)
    cs[...] = jnp.broadcast_to(jnp.sum(inv * imp_ref[...], axis=1, keepdims=True), (LEV, W))

    for q in range(L):
        lo, at, n = window(q)

        @pl.when(l == q)
        def _(q=q, at=at, n=n):
            for p in range(L):
                remote(
                    p_buf.at[pl.ds(0, n)], part.at[p, pl.ds(at, n)], part_s.at[q], part_r.at[p], (other, h, p)
                ).wait_recv()
            remote(kap_ref.at[pl.ds(0, n)], kapw.at[pl.ds(at, n)], kapw_s, kapw_r, (other, h, q)).wait_recv()
            if q == 0 or q == L - 1:
                at_e = 0 if q == 0 else WIN - MARGIN
                for p in range(L):
                    remote(
                        p_buf.at[pl.ds(0, MARGIN)],
                        part.at[p, pl.ds(at_e, MARGIN)],
                        pedge_s.at[0],
                        pedge_r.at[p],
                        (other, h, p),
                    ).wait_recv()
                remote(
                    kap_ref.at[pl.ds(0, MARGIN)], kapw.at[pl.ds(at_e, MARGIN)], kedge_s, kedge_r, (other, h, q)
                ).wait_recv()

    total = part[0]
    for p in range(1, L):
        total = total + part[p]
    surface = diffuse(total, staged(kapw[...], steps_other)).astype(BF16)

    first_row = (h * L + l) * B
    rows_total = H * L * B
    place = rows_ref[...] - first_row + REACH
    place = jnp.where(place < 0, place + rows_total, place)
    place = jnp.where(place >= rows_total, place - rows_total, place) + HALO
    usable = lax.broadcasted_iota(jnp.int32, place.shape, 1) < counts_ref[...]
    place = jnp.where(usable, place, -1)
    cells = lax.broadcasted_iota(jnp.int32, (B, WIN), 1)
    pairs = place.shape[1]
    sources = jnp.concatenate(
        [
            jnp.dot(
                jnp.where(cells == place[:, j : j + 1], 1.0, 0.0).astype(BF16),
                surface,
                preferred_element_type=F32,
            ).astype(BF16)
            for j in range(pairs)
        ],
        axis=1,
    )
    w_copy.wait()
    row_of = lax.broadcasted_iota(jnp.int32, (B, W), 0)
    forcing = jnp.zeros((B, W), F32)
    for r in range(B):
        product = jnp.dot(sources, w_buf[r * pairs * W : (r + 1) * pairs * W, :], preferred_element_type=F32)
        forcing = jnp.where(row_of == r, product, forcing)
    f_ref[...] = forcing
    fm[l] = forcing * mask_ref[...].astype(F32)

    def fm_copy(d, slot):
        peer = lax.rem(l + d, L)
        return remote(fm.at[slot], fm.at[slot], fm_s.at[d - 1], fm_r.at[slot], (s, h, peer))

    for d in range(1, L):
        fm_copy(d, l).start()

    for q in range(L):

        @pl.when(l != q)
        def _(q=q):
            bulk_copy(q, q).wait_recv()

    def ret_copy(q, t, slot):
        return remote(y16.at[q, t], yr.at[slot, t], ret_s.at[q, t], ret_r.at[slot, t], (s, h, q))

    for t in range(T):
        for q in range(L):
            c_buf[t, q * K * 8 : (q + 1) * K * 8, :] = col16[q, t].astype(F32).reshape(K * 8, W)
        for r in range(0, 8, 2):
            x = jnp.concatenate(
                [c_buf[t, pl.ds(r + e, LEV, stride=8), :] for e in range(2)], axis=1
            ).astype(BF16)
            y = jnp.dot(mix_hi, x, preferred_element_type=F32) + jnp.dot(
                mix_lo, x, preferred_element_type=F32
            )
            for e in range(2):
                z_buf[t, pl.ds(r + e, LEV, stride=8), :] = y[:, e * W : (e + 1) * W]
        for q in range(L):
            y16[q, t] = z_buf[t, q * K * 8 : (q + 1) * K * 8, :].reshape(G, 16, W).astype(BF16)
        for q in range(L):

            @pl.when(l != q)
            def _(q=q, t=t):
                ret_copy(q, t, l).start()

            @pl.when(l == q)
            def _(q=q, t=t):
                yr[q, t] = y16[q, t]

    for d in range(1, L):
        fm_copy(d, lax.rem(l + d, L)).wait_recv()

    for t in range(T):
        for q in range(L):

            @pl.when(l != q)
            def _(q=q, t=t):
                ret_copy(q, t, q).wait_recv()

        def finish(g, _, t=t):
            for e in range(2):
                k = 2 * g + e
                c = cs[pl.ds(l * K + k, 1), :]
                for q in range(L):
                    at = q * B + 8 * t
                    y = yr[q, t, g].astype(F32)[8 * e : 8 * e + 8]
                    out_ref[k, at : at + 8, :] = out_ref[k, at : at + 8, :] + (
                        y + c * fm[q, 8 * t : 8 * t + 8, :]
                    )
            return 0

        lax.fori_loop(0, G, finish, 0)

    for c in halos:
        c.wait_send()
    for q in range(L):
        part_copy(q).wait_send()

        @pl.when(l == q)
        def _(q=q):
            kap_copy(q).wait_send()

        @pl.when(l != q)
        def _(q=q):
            bulk_copy(q, l).wait_send()
            for t in range(T):
                ret_copy(q, t, l).wait_send()

    edge_low.wait_send()
    edge_high.wait_send()

    @pl.when(l == 0)
    def _():
        kedge_low.wait_send()

    @pl.when(l == L - 1)
    def _():
        kedge_high.wait_send()

    for d in range(1, L):
        fm_copy(d, l).wait_send()


def per_device(
    state,
    diffusivity,
    coupling_mask,
    pair_rows,
    pair_counts,
    remap_weights,
    export_profile,
    import_profile,
    column_inverse,
):
    _, K, R, W = state.shape
    H = lax.axis_size("horiz")
    L = lax.axis_size("lev")
    B = R // L
    T = B // 8
    G = K // 2
    WIN = B + 2 * MARGIN
    LEV = K * L
    pairs = pair_rows.shape[2]
    weights = remap_weights.reshape(B * pairs * W, W)
    vmem = pl.BlockSpec(memory_space=pltpu.VMEM)
    smem = pl.BlockSpec(memory_space=pltpu.SMEM)
    hbm = pl.BlockSpec(memory_space=pl.ANY)
    dma = pltpu.SemaphoreType.DMA
    new_state, forcing = pl.pallas_call(
        functools.partial(kernel, (H, L, K, R, W)),
        out_shape=(jax.ShapeDtypeStruct((K, R, W), F32), jax.ShapeDtypeStruct((B, W), F32)),
        in_specs=[vmem, vmem, vmem, vmem, vmem, hbm, smem, vmem, vmem],
        out_specs=(vmem, vmem),
        scratch_shapes=[
            pltpu.VMEM(weights.shape, BF16),
            pltpu.VMEM((R, W), F32),
            pltpu.VMEM((L, WIN, W), F32),
            pltpu.VMEM((WIN, W), F32),
            pltpu.VMEM((2, K, HALO, W), F32),
            pltpu.VMEM((2, HALO, W), F32),
            pltpu.VMEM((L, T, G, 16, W), BF16),
            pltpu.VMEM((L, T, G, 16, W), BF16),
            pltpu.VMEM((T, LEV * 8, W), F32),
            pltpu.VMEM((T, LEV * 8, W), F32),
            pltpu.VMEM((L, T, G, 16, W), BF16),
            pltpu.VMEM((L, T, G, 16, W), BF16),
            pltpu.VMEM((L, B, W), F32),
            pltpu.VMEM((LEV, W), F32),
            dma,
            dma((2,)),
            dma((2,)),
            dma((2,)),
            dma((2,)),
            dma((L,)),
            dma((L,)),
            dma((2,)),
            dma((L,)),
            dma,
            dma,
            dma,
            dma,
            dma((L,)),
            dma((L,)),
            dma((L - 1,)),
            dma((L,)),
            dma((L, T)),
            dma((L, T)),
        ],
        compiler_params=pltpu.CompilerParams(
            collective_id=0, has_side_effects=True, vmem_limit_bytes=40 * 1024 * 1024
        ),
    )(
        state[0],
        diffusivity[0],
        coupling_mask[0],
        pair_rows[0],
        pair_counts.reshape(B, 1),
        weights,
        export_profile,
        import_profile,
        column_inverse[0],
    )
    return (new_state[None], forcing[None])


def solution(mesh):
    placed = (
        P("sec", "lev", "horiz", None),
        P("sec", "horiz", None),
        P("sec", ("horiz", "lev"), None),
        P("sec", ("horiz", "lev"), None),
        P("sec", ("horiz", "lev")),
        P("sec", ("horiz", "lev"), None, None, None),
        P("sec", None),
        P("sec", None),
        P("sec", None, None),
    )
    return jax.shard_map(
        per_device,
        mesh=mesh,
        in_specs=placed,
        out_specs=(P("sec", "lev", "horiz", None), P("sec", ("horiz", "lev"), None)),
        check_vma=False,
    )
```

```python
import functools

import jax
import jax.numpy as jnp
from jax import lax
from jax.experimental import pallas as pl
from jax.experimental.pallas import tpu as pltpu
from jax.sharding import PartitionSpec as P

REACH = 8
ATM_STEPS = 4
OCN_STEPS = 2
HALO = 8
MARGIN = REACH + HALO
F32 = jnp.float32
BF16 = jnp.bfloat16


def diffuse(v, kappas):
    rows = v.shape[0]
    for k in kappas:
        around = (
            pltpu.roll(v, 1, 0)
            + pltpu.roll(v, rows - 1, 0)
            + pltpu.roll(v, 1, 1)
            + pltpu.roll(v, v.shape[1] - 1, 1)
        )
        v = v + k * (around - 4.0 * v)
    return v


def kernel(
    sizes,
    x_hbm,
    kap_hbm,
    mask_hbm,
    rows_hbm,
    counts_hbm,
    w_hbm,
    exp_hbm,
    imp_hbm,
    inv_hbm,
    out_ref,
    f_ref,
    x_ref,
    kap_ref,
    mask_ref,
    rows_ref,
    counts_ref,
    w_buf,
    exp_ref,
    imp_ref,
    inv_ref,
    p_buf,
    part,
    kapw,
    halo_x,
    halo_k,
    dyn16,
    col16,
    c_buf,
    z_buf,
    y16,
    yr,
    fm,
    cs,
    in_sem,
    halo_s,
    halo_r,
    halok_s,
    halok_r,
    part_s,
    part_r,
    pedge_s,
    pedge_r,
    kapw_s,
    kapw_r,
    kedge_s,
    kedge_r,
    bulk_s,
    bulk_r,
    fm_s,
    fm_r,
    ret_s,
    ret_r,
):
    H, L, K, R, W = sizes
    B = R // L
    T = B // 8
    G = K // 2
    WIN = B + 2 * MARGIN
    LEV = K * L
    s = lax.axis_index("sec")
    h = lax.axis_index("horiz")
    l = lax.axis_index("lev")
    other = 1 - s
    nxt = lax.rem(h + 1, H)
    prv = lax.rem(h + H - 1, H)

    def remote(src, dst, ssem, rsem, dev):
        return pltpu.make_async_remote_copy(
            src_ref=src,
            dst_ref=dst,
            send_sem=ssem,
            recv_sem=rsem,
            device_id=dev,
            device_id_type=pl.DeviceIdType.MESH,
        )

    loads = [
        pltpu.make_async_copy(src, dst, in_sem.at[i])
        for i, (src, dst) in enumerate(
            (
                (x_hbm, x_ref),
                (exp_hbm, exp_ref),
                (kap_hbm, kap_ref),
                (inv_hbm, inv_ref),
                (imp_hbm, imp_ref),
                (rows_hbm, rows_ref),
                (counts_hbm, counts_ref),
                (mask_hbm, mask_ref),
                (w_hbm, w_buf),
            )
        )
    ]
    for c in loads:
        c.start()

    barrier = pltpu.get_barrier_semaphore()

    def greet(dev):
        pl.semaphore_signal(barrier, inc=1, device_id=dev, device_id_type=pl.DeviceIdType.MESH)

    for d in range(1, L):
        greet((s, h, lax.rem(l + d, L)))
    greet((s, nxt, l))
    greet((s, prv, l))
    for q in range(L):
        greet((other, h, q))

    @pl.when(l == 0)
    def _():
        for q in range(L):
            greet((other, prv, q))

    @pl.when(l == L - 1)
    def _():
        for q in range(L):
            greet((other, nxt, q))

    loads[0].wait()
    loads[1].wait()

    def add_level(k, acc):
        return acc + exp_ref[0, l * K + k] * x_ref[k]

    p_buf[...] = lax.fori_loop(0, K, add_level, jnp.zeros((R, W), F32), unroll=4)

    loads[2].wait()
    pl.semaphore_wait(barrier, (L - 1) + 2 + L + 2)

    halos = [
        remote(x_ref.at[:, pl.ds(R - HALO, HALO)], halo_x.at[0], halo_s.at[0], halo_r.at[0], (s, nxt, l)),
        remote(x_ref.at[:, pl.ds(0, HALO)], halo_x.at[1], halo_s.at[1], halo_r.at[1], (s, prv, l)),
        remote(kap_ref.at[pl.ds(R - HALO, HALO)], halo_k.at[0], halok_s.at[0], halok_r.at[0], (s, nxt, l)),
        remote(kap_ref.at[pl.ds(0, HALO)], halo_k.at[1], halok_s.at[1], halok_r.at[1], (s, prv, l)),
    ]
    for c in halos:
        c.start()

    def window(q):
        lo = max(q * B - MARGIN, 0)
        hi = min(q * B + B + MARGIN, R)
        return lo, lo - (q * B - MARGIN), hi - lo

    def part_copy(q):
        lo, at, n = window(q)
        return remote(
            p_buf.at[pl.ds(lo, n)], part.at[l, pl.ds(at, n)], part_s.at[q], part_r.at[l], (other, h, q)
        )

    def kap_copy(q):
        lo, at, n = window(q)
        return remote(kap_ref.at[pl.ds(lo, n)], kapw.at[pl.ds(at, n)], kapw_s, kapw_r, (other, h, q))

    edge_low = remote(
        p_buf.at[pl.ds(R - MARGIN, MARGIN)],
        part.at[l, pl.ds(0, MARGIN)],
        pedge_s.at[0],
        pedge_r.at[l],
        (other, nxt, 0),
    )
    edge_high = remote(
        p_buf.at[pl.ds(0, MARGIN)],
        part.at[l, pl.ds(WIN - MARGIN, MARGIN)],
        pedge_s.at[1],
        pedge_r.at[l],
        (other, prv, L - 1),
    )
    kedge_low = remote(
        kap_ref.at[pl.ds(R - MARGIN, MARGIN)], kapw.at[pl.ds(0, MARGIN)], kedge_s, kedge_r, (other, nxt, 0)
    )
    kedge_high = remote(
        kap_ref.at[pl.ds(0, MARGIN)],
        kapw.at[pl.ds(WIN - MARGIN, MARGIN)],
        kedge_s,
        kedge_r,
        (other, prv, L - 1),
    )
    for q in range(L):
        part_copy(q).start()
    edge_low.start()
    edge_high.start()
    for q in range(L):

        @pl.when(l == q)
        def _(q=q):
            kap_copy(q).start()

    @pl.when(l == 0)
    def _():
        kedge_low.start()

    @pl.when(l == L - 1)
    def _():
        kedge_high.start()

    steps = jnp.where(s == 0, ATM_STEPS, OCN_STEPS)
    steps_other = jnp.where(s == 0, OCN_STEPS, ATM_STEPS)

    def staged(k, count):
        return [k if i < OCN_STEPS else jnp.where(i < count, k, 0.0) for i in range(ATM_STEPS)]

    def keep(v, at, first, g, levels):
        for q, row in levels:
            for t in range(T):
                lo = row + 8 * t - first + at
                dyn16[q, t, g] = jnp.concatenate([v[0][lo : lo + 8], v[1][lo : lo + 8]], axis=0).astype(BF16)

    def bulk_copy(q, dst_slot):
        return remote(dyn16.at[q], col16.at[dst_slot], bulk_s.at[q], bulk_r.at[dst_slot], (s, h, q))

    def send_bulk(q):
        @pl.when(l != q)
        def _():
            bulk_copy(q, l).start()

        @pl.when(l == q)
        def _():
            col16[q] = dyn16[q]

    lo_c, hi_c = B - HALO, R - B + HALO
    k_mid = staged(kap_ref[lo_c:hi_c], steps)

    def middle(g, _):
        v = [diffuse(x_ref[2 * g + e, lo_c:hi_c, :], k_mid) for e in range(2)]
        for e in range(2):
            out_ref[2 * g + e, B : R - B, :] = v[e][HALO : HALO + R - 2 * B]
        keep(v, 0, lo_c, g, [(q, q * B) for q in range(1, L - 1)])
        return 0

    lax.fori_loop(0, G, middle, 0)
    for q in range(1, L - 1):
        send_bulk(q)

    for c in halos:
        c.wait_recv()

    k_top = staged(jnp.concatenate([halo_k[0], kap_ref[0 : B + HALO]], axis=0), steps)

    def top(g, _):
        v = [
            diffuse(jnp.concatenate([halo_x[0, 2 * g + e], x_ref[2 * g + e, 0 : B + HALO, :]], axis=0), k_top)
            for e in range(2)
        ]
        for e in range(2):
            out_ref[2 * g + e, 0:B, :] = v[e][HALO : HALO + B]
        keep(v, HALO, 0, g, [(0, 0)])
        return 0

    lax.fori_loop(0, G, top, 0)
    send_bulk(0)

    k_bot = staged(jnp.concatenate([kap_ref[R - B - HALO : R], halo_k[1]], axis=0), steps)

    def bottom(g, _):
        v = [
            diffuse(
                jnp.concatenate([x_ref[2 * g + e, R - B - HALO : R, :], halo_x[1, 2 * g + e]], axis=0), k_bot
            )
            for e in range(2)
        ]
        for e in range(2):
            out_ref[2 * g + e, R - B : R, :] = v[e][HALO : HALO + B]
        keep(v, HALO, R - B, g, [(L - 1, R - B)])
        return 0

    lax.fori_loop(0, G, bottom, 0)
    send_bulk(L - 1)

    for c in loads[3:8]:
        c.wait()
    inv = inv_ref[...]
    first = lax.broadcasted_iota(jnp.int32, (LEV, LEV), 0)
    second = lax.broadcasted_iota(jnp.int32, (LEV, LEV), 1)
    mix = inv - jnp.where(first == second, 1.0, 0.0)
    mix_hi = mix.astype(BF16)
    mix_lo = (mix - mix_hi.astype(F32)).astype(BF16)
    cs[...] = jnp.broadcast_to(jnp.sum(inv * imp_ref[...], axis=1, keepdims=True), (LEV, W))

    for q in range(L):
        lo, at, n = window(q)

        @pl.when(l == q)
        def _(q=q, at=at, n=n):
            for p in range(L):
                remote(
                    p_buf.at[pl.ds(0, n)], part.at[p, pl.ds(at, n)], part_s.at[q], part_r.at[p], (other, h, p)
                ).wait_recv()
            remote(kap_ref.at[pl.ds(0, n)], kapw.at[pl.ds(at, n)], kapw_s, kapw_r, (other, h, q)).wait_recv()
            if q == 0 or q == L - 1:
                at_e = 0 if q == 0 else WIN - MARGIN
                for p in range(L):
                    remote(
                        p_buf.at[pl.ds(0, MARGIN)],
                        part.at[p, pl.ds(at_e, MARGIN)],
                        pedge_s.at[0],
                        pedge_r.at[p],
                        (other, h, p),
                    ).wait_recv()
                remote(
                    kap_ref.at[pl.ds(0, MARGIN)], kapw.at[pl.ds(at_e, MARGIN)], kedge_s, kedge_r, (other, h, q)
                ).wait_recv()

    total = part[0]
    for p in range(1, L):
        total = total + part[p]
    surface = diffuse(total, staged(kapw[...], steps_other)).astype(BF16)

    first_row = (h * L + l) * B
    rows_total = H * L * B
    place = rows_ref[...] - first_row + REACH
    place = jnp.where(place < 0, place + rows_total, place)
    place = jnp.where(place >= rows_total, place - rows_total, place) + HALO
    pairs = place.shape[0]
    counts = counts_ref[...]
    cells = lax.broadcasted_iota(jnp.int32, (WIN, B), 0)
    sources = jnp.concatenate(
        [
            lax.dot_general(
                jnp.where((cells == place[j]) & (counts > j), 1.0, 0.0).astype(BF16),
                surface,
                (((0,), (0,)), ((), ())),
                preferred_element_type=F32,
            ).astype(BF16)
            for j in range(pairs)
        ],
        axis=1,
    )
    loads[8].wait()
    row_of = lax.broadcasted_iota(jnp.int32, (B, W), 0)
    forcing = jnp.zeros((B, W), F32)
    for r in range(B):
        product = jnp.dot(sources, w_buf[r * pairs * W : (r + 1) * pairs * W, :], preferred_element_type=F32)
        forcing = jnp.where(row_of == r, product, forcing)
    f_ref[...] = forcing
    fm[l] = forcing * mask_ref[...].astype(F32)

    def fm_copy(d, slot):
        peer = lax.rem(l + d, L)
        return remote(fm.at[slot], fm.at[slot], fm_s.at[d - 1], fm_r.at[slot], (s, h, peer))

    for d in range(1, L):
        fm_copy(d, l).start()

    for q in range(L):

        @pl.when(l != q)
        def _(q=q):
            bulk_copy(q, q).wait_recv()

    def ret_copy(q, t, slot):
        return remote(y16.at[q, t], yr.at[slot, t], ret_s.at[q, t], ret_r.at[slot, t], (s, h, q))

    for t in range(T):
        for q in range(L):
            c_buf[t, q * K * 8 : (q + 1) * K * 8, :] = col16[q, t].astype(F32).reshape(K * 8, W)
        for r in range(0, 8, 2):
            x = jnp.concatenate(
                [c_buf[t, pl.ds(r + e, LEV, stride=8), :] for e in range(2)], axis=1
            ).astype(BF16)
            y = jnp.dot(mix_hi, x, preferred_element_type=F32) + jnp.dot(
                mix_lo, x, preferred_element_type=F32
            )
            for e in range(2):
                z_buf[t, pl.ds(r + e, LEV, stride=8), :] = y[:, e * W : (e + 1) * W]
        for q in range(L):
            y16[q, t] = z_buf[t, q * K * 8 : (q + 1) * K * 8, :].reshape(G, 16, W).astype(BF16)
        for q in range(L):

            @pl.when(l != q)
            def _(q=q, t=t):
                ret_copy(q, t, l).start()

            @pl.when(l == q)
            def _(q=q, t=t):
                yr[q, t] = y16[q, t]

    for d in range(1, L):
        fm_copy(d, lax.rem(l + d, L)).wait_recv()

    for t in range(T):
        for q in range(L):

            @pl.when(l != q)
            def _(q=q, t=t):
                ret_copy(q, t, q).wait_recv()

        def finish(g, _, t=t):
            for e in range(2):
                k = 2 * g + e
                c = cs[pl.ds(l * K + k, 1), :]
                for q in range(L):
                    at = q * B + 8 * t
                    y = yr[q, t, g].astype(F32)[8 * e : 8 * e + 8]
                    out_ref[k, at : at + 8, :] = out_ref[k, at : at + 8, :] + (
                        y + c * fm[q, 8 * t : 8 * t + 8, :]
                    )
            return 0

        lax.fori_loop(0, G, finish, 0)

    for c in halos:
        c.wait_send()
    for q in range(L):
        part_copy(q).wait_send()

        @pl.when(l == q)
        def _(q=q):
            kap_copy(q).wait_send()

        @pl.when(l != q)
        def _(q=q):
            bulk_copy(q, l).wait_send()
            for t in range(T):
                ret_copy(q, t, l).wait_send()

    edge_low.wait_send()
    edge_high.wait_send()

    @pl.when(l == 0)
    def _():
        kedge_low.wait_send()

    @pl.when(l == L - 1)
    def _():
        kedge_high.wait_send()

    for d in range(1, L):
        fm_copy(d, l).wait_send()


def per_device(
    state,
    diffusivity,
    coupling_mask,
    pair_rows,
    pair_counts,
    remap_weights,
    export_profile,
    import_profile,
    column_inverse,
):
    _, K, R, W = state.shape
    H = lax.axis_size("horiz")
    L = lax.axis_size("lev")
    B = R // L
    T = B // 8
    G = K // 2
    WIN = B + 2 * MARGIN
    LEV = K * L
    pairs = pair_rows.shape[2]
    weights = remap_weights.reshape(B * pairs * W, W)
    vmem = pl.BlockSpec(memory_space=pltpu.VMEM)
    hbm = pl.BlockSpec(memory_space=pltpu.HBM)
    dma = pltpu.SemaphoreType.DMA
    new_state, forcing = pl.pallas_call(
        functools.partial(kernel, (H, L, K, R, W)),
        out_shape=(jax.ShapeDtypeStruct((K, R, W), F32), jax.ShapeDtypeStruct((B, W), F32)),
        in_specs=[hbm] * 9,
        out_specs=(vmem, vmem),
        scratch_shapes=[
            pltpu.VMEM((K, R, W), F32),
            pltpu.VMEM((R, W), F32),
            pltpu.VMEM((B, W), jnp.int32),
            pltpu.VMEM((pairs, 1, B), jnp.int32),
            pltpu.VMEM((1, B), jnp.int32),
            pltpu.VMEM(weights.shape, BF16),
            pltpu.SMEM((1, LEV), F32),
            pltpu.VMEM((1, LEV), F32),
            pltpu.VMEM((LEV, LEV), F32),
            pltpu.VMEM((R, W), F32),
            pltpu.VMEM((L, WIN, W), F32),
            pltpu.VMEM((WIN, W), F32),
            pltpu.VMEM((2, K, HALO, W), F32),
            pltpu.VMEM((2, HALO, W), F32),
            pltpu.VMEM((L, T, G, 16, W), BF16),
            pltpu.VMEM((L, T, G, 16, W), BF16),
            pltpu.VMEM((T, LEV * 8, W), F32),
            pltpu.VMEM((T, LEV * 8, W), F32),
            pltpu.VMEM((L, T, G, 16, W), BF16),
            pltpu.VMEM((L, T, G, 16, W), BF16),
            pltpu.VMEM((L, B, W), F32),
            pltpu.VMEM((LEV, W), F32),
            dma((9,)),
            dma((2,)),
            dma((2,)),
            dma((2,)),
            dma((2,)),
            dma((L,)),
            dma((L,)),
            dma((2,)),
            dma((L,)),
            dma,
            dma,
            dma,
            dma,
            dma((L,)),
            dma((L,)),
            dma((L - 1,)),
            dma((L,)),
            dma((L, T)),
            dma((L, T)),
        ],
        compiler_params=pltpu.CompilerParams(
            collective_id=0, has_side_effects=True, vmem_limit_bytes=56 * 1024 * 1024
        ),
    )(
        state[0],
        diffusivity[0],
        coupling_mask[0],
        jnp.transpose(pair_rows, (2, 0, 1)),
        pair_counts,
        weights,
        export_profile,
        import_profile,
        column_inverse[0],
    )
    return (new_state[None], forcing[None])


def solution(mesh):
    placed = (
        P("sec", "lev", "horiz", None),
        P("sec", "horiz", None),
        P("sec", ("horiz", "lev"), None),
        P("sec", ("horiz", "lev"), None),
        P("sec", ("horiz", "lev")),
        P("sec", ("horiz", "lev"), None, None, None),
        P("sec", None),
        P("sec", None),
        P("sec", None, None),
    )
    return jax.shard_map(
        per_device,
        mesh=mesh,
        in_specs=placed,
        out_specs=(P("sec", "lev", "horiz", None), P("sec", ("horiz", "lev"), None)),
        check_vma=False,
    )
```

```python
import functools

import jax
import jax.numpy as jnp
from jax import lax
from jax.experimental import pallas as pl
from jax.experimental.pallas import tpu as pltpu
from jax.sharding import PartitionSpec as P

REACH = 8
ATM_STEPS = 4
OCN_STEPS = 2
HALO = 8
MARGIN = REACH + HALO
F32 = jnp.float32
BF16 = jnp.bfloat16


def diffuse(v, kappas):
    rows = v.shape[0]
    for k in kappas:
        around = (
            pltpu.roll(v, 1, 0)
            + pltpu.roll(v, rows - 1, 0)
            + pltpu.roll(v, 1, 1)
            + pltpu.roll(v, v.shape[1] - 1, 1)
        )
        v = v + k * (around - 4.0 * v)
    return v


def kernel(
    sizes,
    x_hbm,
    kap_hbm,
    mask_hbm,
    rows_hbm,
    counts_hbm,
    w_hbm,
    exp_hbm,
    imp_hbm,
    inv_hbm,
    out_ref,
    f_ref,
    x_ref,
    kap_ref,
    mask_ref,
    rows_ref,
    counts_ref,
    w_buf,
    exp_ref,
    imp_ref,
    inv_ref,
    p_buf,
    part,
    kapw,
    halo_x,
    halo_k,
    dyn16,
    col16,
    c_buf,
    z_buf,
    y16,
    yr,
    fm,
    cs,
    in_sem,
    halo_s,
    halo_r,
    halok_s,
    halok_r,
    part_s,
    part_r,
    pedge_s,
    pedge_r,
    kapw_s,
    kapw_r,
    kedge_s,
    kedge_r,
    bulk_s,
    bulk_r,
    fm_s,
    fm_r,
    ret_s,
    ret_r,
):
    H, L, K, R, W = sizes
    B = R // L
    T = B // 8
    G = K // 2
    WIN = B + 2 * MARGIN
    LEV = K * L
    s = lax.axis_index("sec")
    h = lax.axis_index("horiz")
    l = lax.axis_index("lev")
    other = 1 - s
    nxt = lax.rem(h + 1, H)
    prv = lax.rem(h + H - 1, H)

    def remote(src, dst, ssem, rsem, dev):
        return pltpu.make_async_remote_copy(
            src_ref=src,
            dst_ref=dst,
            send_sem=ssem,
            recv_sem=rsem,
            device_id=dev,
            device_id_type=pl.DeviceIdType.MESH,
        )

    loads = [
        pltpu.make_async_copy(src, dst, in_sem.at[i])
        for i, (src, dst) in enumerate(
            (
                (x_hbm, x_ref),
                (exp_hbm, exp_ref),
                (kap_hbm, kap_ref),
                (inv_hbm, inv_ref),
                (imp_hbm, imp_ref),
                (rows_hbm, rows_ref),
                (counts_hbm, counts_ref),
                (mask_hbm, mask_ref),
                (w_hbm, w_buf),
            )
        )
    ]
    for c in loads:
        c.start()

    barrier = pltpu.get_barrier_semaphore()

    def greet(dev):
        pl.semaphore_signal(barrier, inc=1, device_id=dev, device_id_type=pl.DeviceIdType.MESH)

    for d in range(1, L):
        greet((s, h, lax.rem(l + d, L)))
    greet((s, nxt, l))
    greet((s, prv, l))
    for q in range(L):
        greet((other, h, q))

    @pl.when(l == 0)
    def _():
        for q in range(L):
            greet((other, prv, q))

    @pl.when(l == L - 1)
    def _():
        for q in range(L):
            greet((other, nxt, q))

    loads[0].wait()
    loads[1].wait()

    def add_level(k, acc):
        return acc + exp_ref[0, l * K + k] * x_ref[k]

    p_buf[...] = lax.fori_loop(0, K, add_level, jnp.zeros((R, W), F32), unroll=4)

    loads[2].wait()
    pl.semaphore_wait(barrier, (L - 1) + 2 + L + 2)

    halos = [
        remote(x_ref.at[:, pl.ds(R - HALO, HALO)], halo_x.at[0], halo_s.at[0], halo_r.at[0], (s, nxt, l)),
        remote(x_ref.at[:, pl.ds(0, HALO)], halo_x.at[1], halo_s.at[1], halo_r.at[1], (s, prv, l)),
        remote(kap_ref.at[pl.ds(R - HALO, HALO)], halo_k.at[0], halok_s.at[0], halok_r.at[0], (s, nxt, l)),
        remote(kap_ref.at[pl.ds(0, HALO)], halo_k.at[1], halok_s.at[1], halok_r.at[1], (s, prv, l)),
    ]
    for c in halos:
        c.start()

    def window(q):
        lo = max(q * B - MARGIN, 0)
        hi = min(q * B + B + MARGIN, R)
        return lo, lo - (q * B - MARGIN), hi - lo

    def part_copy(q):
        lo, at, n = window(q)
        return remote(
            p_buf.at[pl.ds(lo, n)], part.at[l, pl.ds(at, n)], part_s.at[q], part_r.at[l], (other, h, q)
        )

    def kap_copy(q):
        lo, at, n = window(q)
        return remote(kap_ref.at[pl.ds(lo, n)], kapw.at[pl.ds(at, n)], kapw_s, kapw_r, (other, h, q))

    edge_low = remote(
        p_buf.at[pl.ds(R - MARGIN, MARGIN)],
        part.at[l, pl.ds(0, MARGIN)],
        pedge_s.at[0],
        pedge_r.at[l],
        (other, nxt, 0),
    )
    edge_high = remote(
        p_buf.at[pl.ds(0, MARGIN)],
        part.at[l, pl.ds(WIN - MARGIN, MARGIN)],
        pedge_s.at[1],
        pedge_r.at[l],
        (other, prv, L - 1),
    )
    kedge_low = remote(
        kap_ref.at[pl.ds(R - MARGIN, MARGIN)], kapw.at[pl.ds(0, MARGIN)], kedge_s, kedge_r, (other, nxt, 0)
    )
    kedge_high = remote(
        kap_ref.at[pl.ds(0, MARGIN)],
        kapw.at[pl.ds(WIN - MARGIN, MARGIN)],
        kedge_s,
        kedge_r,
        (other, prv, L - 1),
    )
    for q in range(L):
        part_copy(q).start()
    edge_low.start()
    edge_high.start()
    for q in range(L):

        @pl.when(l == q)
        def _(q=q):
            kap_copy(q).start()

    @pl.when(l == 0)
    def _():
        kedge_low.start()

    @pl.when(l == L - 1)
    def _():
        kedge_high.start()

    steps = jnp.where(s == 0, ATM_STEPS, OCN_STEPS)
    steps_other = jnp.where(s == 0, OCN_STEPS, ATM_STEPS)

    def staged(k, count):
        return [k if i < OCN_STEPS else jnp.where(i < count, k, 0.0) for i in range(ATM_STEPS)]

    def keep(v, at, first, g, levels):
        for q, row in levels:
            for t in range(T):
                lo = row + 8 * t - first + at
                dyn16[q, t, g] = jnp.concatenate([v[0][lo : lo + 8], v[1][lo : lo + 8]], axis=0).astype(BF16)

    def bulk_copy(q, dst_slot):
        return remote(dyn16.at[q], col16.at[dst_slot], bulk_s.at[q], bulk_r.at[dst_slot], (s, h, q))

    def send_bulk(q):
        @pl.when(l != q)
        def _():
            bulk_copy(q, l).start()

        @pl.when(l == q)
        def _():
            col16[q] = dyn16[q]

    lo_c, hi_c = B - HALO, R - B + HALO
    k_mid = staged(kap_ref[lo_c:hi_c], steps)

    def middle(g, _):
        v = [diffuse(x_ref[2 * g + e, lo_c:hi_c, :], k_mid) for e in range(2)]
        for e in range(2):
            out_ref[2 * g + e, B : R - B, :] = v[e][HALO : HALO + R - 2 * B]
        keep(v, 0, lo_c, g, [(q, q * B) for q in range(1, L - 1)])
        return 0

    lax.fori_loop(0, G, middle, 0, unroll=5 if G % 5 == 0 else 1)
    for q in range(1, L - 1):
        send_bulk(q)

    for c in halos:
        c.wait_recv()

    k_top = staged(jnp.concatenate([halo_k[0], kap_ref[0 : B + HALO]], axis=0), steps)

    def top(g, _):
        v = [
            diffuse(jnp.concatenate([halo_x[0, 2 * g + e], x_ref[2 * g + e, 0 : B + HALO, :]], axis=0), k_top)
            for e in range(2)
        ]
        for e in range(2):
            out_ref[2 * g + e, 0:B, :] = v[e][HALO : HALO + B]
        keep(v, HALO, 0, g, [(0, 0)])
        return 0

    lax.fori_loop(0, G, top, 0, unroll=5 if G % 5 == 0 else 1)
    send_bulk(0)

    k_bot = staged(jnp.concatenate([kap_ref[R - B - HALO : R], halo_k[1]], axis=0), steps)

    def bottom(g, _):
        v = [
            diffuse(
                jnp.concatenate([x_ref[2 * g + e, R - B - HALO : R, :], halo_x[1, 2 * g + e]], axis=0), k_bot
            )
            for e in range(2)
        ]
        for e in range(2):
            out_ref[2 * g + e, R - B : R, :] = v[e][HALO : HALO + B]
        keep(v, HALO, R - B, g, [(L - 1, R - B)])
        return 0

    lax.fori_loop(0, G, bottom, 0, unroll=5 if G % 5 == 0 else 1)
    send_bulk(L - 1)

    for c in loads[3:8]:
        c.wait()
    inv = inv_ref[...]
    first = lax.broadcasted_iota(jnp.int32, (LEV, LEV), 0)
    second = lax.broadcasted_iota(jnp.int32, (LEV, LEV), 1)
    mix = inv - jnp.where(first == second, 1.0, 0.0)
    mix_hi = mix.astype(BF16)
    mix_lo = (mix - mix_hi.astype(F32)).astype(BF16)
    cs[...] = jnp.broadcast_to(jnp.sum(inv * imp_ref[...], axis=1, keepdims=True), (LEV, W))

    for q in range(L):
        lo, at, n = window(q)

        @pl.when(l == q)
        def _(q=q, at=at, n=n):
            for p in range(L):
                remote(
                    p_buf.at[pl.ds(0, n)], part.at[p, pl.ds(at, n)], part_s.at[q], part_r.at[p], (other, h, p)
                ).wait_recv()
            remote(kap_ref.at[pl.ds(0, n)], kapw.at[pl.ds(at, n)], kapw_s, kapw_r, (other, h, q)).wait_recv()
            if q == 0 or q == L - 1:
                at_e = 0 if q == 0 else WIN - MARGIN
                for p in range(L):
                    remote(
                        p_buf.at[pl.ds(0, MARGIN)],
                        part.at[p, pl.ds(at_e, MARGIN)],
                        pedge_s.at[0],
                        pedge_r.at[p],
                        (other, h, p),
                    ).wait_recv()
                remote(
                    kap_ref.at[pl.ds(0, MARGIN)], kapw.at[pl.ds(at_e, MARGIN)], kedge_s, kedge_r, (other, h, q)
                ).wait_recv()

    total = part[0]
    for p in range(1, L):
        total = total + part[p]
    surface = diffuse(total, staged(kapw[...], steps_other)).astype(BF16)

    first_row = (h * L + l) * B
    rows_total = H * L * B
    place = rows_ref[...] - first_row + REACH
    place = jnp.where(place < 0, place + rows_total, place)
    place = jnp.where(place >= rows_total, place - rows_total, place) + HALO
    pairs = place.shape[0]
    counts = counts_ref[...]
    cells = lax.broadcasted_iota(jnp.int32, (WIN, B), 0)
    sources = jnp.concatenate(
        [
            lax.dot_general(
                jnp.where((cells == place[j]) & (counts > j), 1.0, 0.0).astype(BF16),
                surface,
                (((0,), (0,)), ((), ())),
                preferred_element_type=F32,
            ).astype(BF16)
            for j in range(pairs)
        ],
        axis=1,
    )
    loads[8].wait()
    row_of = lax.broadcasted_iota(jnp.int32, (B, W), 0)
    forcing = jnp.zeros((B, W), F32)
    for r in range(B):
        product = jnp.dot(sources, w_buf[r * pairs * W : (r + 1) * pairs * W, :], preferred_element_type=F32)
        forcing = jnp.where(row_of == r, product, forcing)
    f_ref[...] = forcing
    fm[l] = forcing * mask_ref[...].astype(F32)

    def fm_copy(d, slot):
        peer = lax.rem(l + d, L)
        return remote(fm.at[slot], fm.at[slot], fm_s.at[d - 1], fm_r.at[slot], (s, h, peer))

    for d in range(1, L):
        fm_copy(d, l).start()

    for q in range(L):

        @pl.when(l != q)
        def _(q=q):
            bulk_copy(q, q).wait_recv()

    def ret_copy(q, t, slot):
        return remote(y16.at[q, t], yr.at[slot, t], ret_s.at[q, t], ret_r.at[slot, t], (s, h, q))

    for t in range(T):
        for q in range(L):
            c_buf[t, q * K * 8 : (q + 1) * K * 8, :] = col16[q, t].astype(F32).reshape(K * 8, W)
        for r in range(0, 8, 2):
            x = jnp.concatenate(
                [c_buf[t, pl.ds(r + e, LEV, stride=8), :] for e in range(2)], axis=1
            ).astype(BF16)
            y = jnp.dot(mix_hi, x, preferred_element_type=F32) + jnp.dot(
                mix_lo, x, preferred_element_type=F32
            )
            for e in range(2):
                z_buf[t, pl.ds(r + e, LEV, stride=8), :] = y[:, e * W : (e + 1) * W]
        for q in range(L):
            y16[q, t] = z_buf[t, q * K * 8 : (q + 1) * K * 8, :].reshape(G, 16, W).astype(BF16)
        for q in range(L):

            @pl.when(l != q)
            def _(q=q, t=t):
                ret_copy(q, t, l).start()

            @pl.when(l == q)
            def _(q=q, t=t):
                yr[q, t] = y16[q, t]

    for d in range(1, L):
        fm_copy(d, lax.rem(l + d, L)).wait_recv()

    for t in range(T):
        for q in range(L):

            @pl.when(l != q)
            def _(q=q, t=t):
                ret_copy(q, t, q).wait_recv()

        def finish(g, _, t=t):
            for e in range(2):
                k = 2 * g + e
                c = cs[pl.ds(l * K + k, 1), :]
                for q in range(L):
                    at = q * B + 8 * t
                    y = yr[q, t, g].astype(F32)[8 * e : 8 * e + 8]
                    out_ref[k, at : at + 8, :] = out_ref[k, at : at + 8, :] + (
                        y + c * fm[q, 8 * t : 8 * t + 8, :]
                    )
            return 0

        lax.fori_loop(0, G, finish, 0)

    for c in halos:
        c.wait_send()
    for q in range(L):
        part_copy(q).wait_send()

        @pl.when(l == q)
        def _(q=q):
            kap_copy(q).wait_send()

        @pl.when(l != q)
        def _(q=q):
            bulk_copy(q, l).wait_send()
            for t in range(T):
                ret_copy(q, t, l).wait_send()

    edge_low.wait_send()
    edge_high.wait_send()

    @pl.when(l == 0)
    def _():
        kedge_low.wait_send()

    @pl.when(l == L - 1)
    def _():
        kedge_high.wait_send()

    for d in range(1, L):
        fm_copy(d, l).wait_send()


def per_device(
    state,
    diffusivity,
    coupling_mask,
    pair_rows,
    pair_counts,
    remap_weights,
    export_profile,
    import_profile,
    column_inverse,
):
    _, K, R, W = state.shape
    H = lax.axis_size("horiz")
    L = lax.axis_size("lev")
    B = R // L
    T = B // 8
    G = K // 2
    WIN = B + 2 * MARGIN
    LEV = K * L
    pairs = pair_rows.shape[2]
    weights = remap_weights.reshape(B * pairs * W, W)
    vmem = pl.BlockSpec(memory_space=pltpu.VMEM)
    hbm = pl.BlockSpec(memory_space=pltpu.HBM)
    dma = pltpu.SemaphoreType.DMA
    new_state, forcing = pl.pallas_call(
        functools.partial(kernel, (H, L, K, R, W)),
        out_shape=(pltpu.VMEM((K, R, W), F32), pltpu.VMEM((B, W), F32)),
        in_specs=[hbm] * 9,
        out_specs=(vmem, vmem),
        scratch_shapes=[
            pltpu.VMEM((K, R, W), F32),
            pltpu.VMEM((R, W), F32),
            pltpu.VMEM((B, W), jnp.int32),
            pltpu.VMEM((pairs, 1, B), jnp.int32),
            pltpu.VMEM((1, B), jnp.int32),
            pltpu.VMEM(weights.shape, BF16),
            pltpu.SMEM((1, LEV), F32),
            pltpu.VMEM((1, LEV), F32),
            pltpu.VMEM((LEV, LEV), F32),
            pltpu.VMEM((R, W), F32),
            pltpu.VMEM((L, WIN, W), F32),
            pltpu.VMEM((WIN, W), F32),
            pltpu.VMEM((2, K, HALO, W), F32),
            pltpu.VMEM((2, HALO, W), F32),
            pltpu.VMEM((L, T, G, 16, W), BF16),
            pltpu.VMEM((L, T, G, 16, W), BF16),
            pltpu.VMEM((T, LEV * 8, W), F32),
            pltpu.VMEM((T, LEV * 8, W), F32),
            pltpu.VMEM((L, T, G, 16, W), BF16),
            pltpu.VMEM((L, T, G, 16, W), BF16),
            pltpu.VMEM((L, B, W), F32),
            pltpu.VMEM((LEV, W), F32),
            dma((9,)),
            dma((2,)),
            dma((2,)),
            dma((2,)),
            dma((2,)),
            dma((L,)),
            dma((L,)),
            dma((2,)),
            dma((L,)),
            dma,
            dma,
            dma,
            dma,
            dma((L,)),
            dma((L,)),
            dma((L - 1,)),
            dma((L,)),
            dma((L, T)),
            dma((L, T)),
        ],
        compiler_params=pltpu.CompilerParams(
            collective_id=0, has_side_effects=True, vmem_limit_bytes=56 * 1024 * 1024
        ),
    )(
        state[0],
        diffusivity[0],
        coupling_mask[0],
        jnp.transpose(pair_rows, (2, 0, 1)),
        pair_counts,
        weights,
        export_profile,
        import_profile,
        column_inverse[0],
    )
    return (new_state[None], forcing[None])


def solution(mesh):
    placed = (
        P("sec", "lev", "horiz", None),
        P("sec", "horiz", None),
        P("sec", ("horiz", "lev"), None),
        P("sec", ("horiz", "lev"), None),
        P("sec", ("horiz", "lev")),
        P("sec", ("horiz", "lev"), None, None, None),
        P("sec", None),
        P("sec", None),
        P("sec", None, None),
    )
    return jax.shard_map(
        per_device,
        mesh=mesh,
        in_specs=placed,
        out_specs=(P("sec", "lev", "horiz", None), P("sec", ("horiz", "lev"), None)),
        check_vma=False,
    )
```

```python
import functools

import jax
import jax.numpy as jnp
from jax import lax
from jax.experimental import pallas as pl
from jax.experimental.pallas import tpu as pltpu
from jax.sharding import PartitionSpec as P

REACH = 8
ATM_STEPS = 4
OCN_STEPS = 2
HALO = 8
MARGIN = REACH + HALO
F32 = jnp.float32
BF16 = jnp.bfloat16


def diffuse(v, kappas):
    rows = v.shape[0]
    for k in kappas:
        around = (
            pltpu.roll(v, 1, 0)
            + pltpu.roll(v, rows - 1, 0)
            + pltpu.roll(v, 1, 1)
            + pltpu.roll(v, v.shape[1] - 1, 1)
        )
        v = v + k * (around - 4.0 * v)
    return v


def kernel(
    sizes,
    x_hbm,
    kap_hbm,
    mask_hbm,
    rows_hbm,
    counts_hbm,
    w_hbm,
    exp_hbm,
    imp_hbm,
    inv_hbm,
    out_ref,
    f_ref,
    x_ref,
    kap_ref,
    mask_ref,
    rows_ref,
    counts_ref,
    w_buf,
    exp_ref,
    imp_ref,
    inv_ref,
    p_buf,
    part,
    kapw,
    halo_x,
    halo_k,
    dyn16,
    col16,
    c_buf,
    z_buf,
    y16,
    yr,
    fm,
    cs,
    in_sem,
    halo_s,
    halo_r,
    halok_s,
    halok_r,
    part_s,
    part_r,
    pedge_s,
    pedge_r,
    kapw_s,
    kapw_r,
    kedge_s,
    kedge_r,
    bulk_s,
    bulk_r,
    fm_s,
    fm_r,
    ret_s,
    ret_r,
):
    H, L, K, R, W = sizes
    B = R // L
    T = B // 8
    G = K // 2
    WIN = B + 2 * MARGIN
    LEV = K * L
    s = lax.axis_index("sec")
    h = lax.axis_index("horiz")
    l = lax.axis_index("lev")
    other = 1 - s
    nxt = lax.rem(h + 1, H)
    prv = lax.rem(h + H - 1, H)

    def remote(src, dst, ssem, rsem, dev):
        return pltpu.make_async_remote_copy(
            src_ref=src,
            dst_ref=dst,
            send_sem=ssem,
            recv_sem=rsem,
            device_id=dev,
            device_id_type=pl.DeviceIdType.MESH,
        )

    loads = [
        pltpu.make_async_copy(src, dst, in_sem.at[i])
        for i, (src, dst) in enumerate(
            (
                (x_hbm, x_ref),
                (exp_hbm, exp_ref),
                (kap_hbm, kap_ref),
                (inv_hbm, inv_ref),
                (imp_hbm, imp_ref),
                (rows_hbm, rows_ref),
                (counts_hbm, counts_ref),
                (mask_hbm, mask_ref),
                (w_hbm, w_buf),
            )
        )
    ]
    for c in loads:
        c.start()

    barrier = pltpu.get_barrier_semaphore()

    def greet(dev):
        pl.semaphore_signal(barrier, inc=1, device_id=dev, device_id_type=pl.DeviceIdType.MESH)

    for d in range(1, L):
        greet((s, h, lax.rem(l + d, L)))
    greet((s, nxt, l))
    greet((s, prv, l))
    for q in range(L):
        greet((other, h, q))

    @pl.when(l == 0)
    def _():
        for q in range(L):
            greet((other, prv, q))

    @pl.when(l == L - 1)
    def _():
        for q in range(L):
            greet((other, nxt, q))

    loads[0].wait()
    loads[1].wait()

    def add_level(k, acc):
        return acc + exp_ref[0, l * K + k] * x_ref[k]

    p_buf[...] = lax.fori_loop(0, K, add_level, jnp.zeros((R, W), F32), unroll=4)

    loads[2].wait()
    pl.semaphore_wait(barrier, (L - 1) + 2 + L + 2)

    halos = [
        remote(x_ref.at[:, pl.ds(R - HALO, HALO)], halo_x.at[0], halo_s.at[0], halo_r.at[0], (s, nxt, l)),
        remote(x_ref.at[:, pl.ds(0, HALO)], halo_x.at[1], halo_s.at[1], halo_r.at[1], (s, prv, l)),
        remote(kap_ref.at[pl.ds(R - HALO, HALO)], halo_k.at[0], halok_s.at[0], halok_r.at[0], (s, nxt, l)),
        remote(kap_ref.at[pl.ds(0, HALO)], halo_k.at[1], halok_s.at[1], halok_r.at[1], (s, prv, l)),
    ]
    for c in halos:
        c.start()

    def window(q):
        lo = max(q * B - MARGIN, 0)
        hi = min(q * B + B + MARGIN, R)
        return lo, lo - (q * B - MARGIN), hi - lo

    def part_copy(q):
        lo, at, n = window(q)
        return remote(
            p_buf.at[pl.ds(lo, n)], part.at[l, pl.ds(at, n)], part_s.at[q], part_r.at[l], (other, h, q)
        )

    def kap_copy(q):
        lo, at, n = window(q)
        return remote(kap_ref.at[pl.ds(lo, n)], kapw.at[pl.ds(at, n)], kapw_s, kapw_r, (other, h, q))

    edge_low = remote(
        p_buf.at[pl.ds(R - MARGIN, MARGIN)],
        part.at[l, pl.ds(0, MARGIN)],
        pedge_s.at[0],
        pedge_r.at[l],
        (other, nxt, 0),
    )
    edge_high = remote(
        p_buf.at[pl.ds(0, MARGIN)],
        part.at[l, pl.ds(WIN - MARGIN, MARGIN)],
        pedge_s.at[1],
        pedge_r.at[l],
        (other, prv, L - 1),
    )
    kedge_low = remote(
        kap_ref.at[pl.ds(R - MARGIN, MARGIN)], kapw.at[pl.ds(0, MARGIN)], kedge_s, kedge_r, (other, nxt, 0)
    )
    kedge_high = remote(
        kap_ref.at[pl.ds(0, MARGIN)],
        kapw.at[pl.ds(WIN - MARGIN, MARGIN)],
        kedge_s,
        kedge_r,
        (other, prv, L - 1),
    )
    for q in range(L):
        part_copy(q).start()
    edge_low.start()
    edge_high.start()
    for q in range(L):

        @pl.when(l == q)
        def _(q=q):
            kap_copy(q).start()

    @pl.when(l == 0)
    def _():
        kedge_low.start()

    @pl.when(l == L - 1)
    def _():
        kedge_high.start()

    steps = jnp.where(s == 0, ATM_STEPS, OCN_STEPS)
    steps_other = jnp.where(s == 0, OCN_STEPS, ATM_STEPS)

    def staged(k, count):
        return [k if i < OCN_STEPS else jnp.where(i < count, k, 0.0) for i in range(ATM_STEPS)]

    def keep(v, at, first, g, levels):
        for q, row in levels:
            for t in range(T):
                lo = row + 8 * t - first + at
                dyn16[q, t, g] = jnp.concatenate([v[0][lo : lo + 8], v[1][lo : lo + 8]], axis=0).astype(BF16)

    half = G // 2 if G % 2 == 0 else G
    parts = G // half

    def bulk_copy(q, dst_slot, i):
        piece = pl.ds(i * half, half)
        return remote(
            dyn16.at[q, :, piece],
            col16.at[dst_slot, :, piece],
            bulk_s.at[q, i],
            bulk_r.at[dst_slot, i],
            (s, h, q),
        )

    def send_bulk(q, i):
        @pl.when(l != q)
        def _():
            bulk_copy(q, l, i).start()

        @pl.when(l == q)
        def _():
            piece = pl.ds(i * half, half)
            col16[q, :, piece] = dyn16[q, :, piece]

    lo_c, hi_c = B - HALO, R - B + HALO
    k_mid = staged(kap_ref[lo_c:hi_c], steps)

    def middle(g, _):
        v = [diffuse(x_ref[2 * g + e, lo_c:hi_c, :], k_mid) for e in range(2)]
        for e in range(2):
            out_ref[2 * g + e, B : R - B, :] = v[e][HALO : HALO + R - 2 * B]
        keep(v, 0, lo_c, g, [(q, q * B) for q in range(1, L - 1)])
        return 0

    for i in range(parts):
        lax.fori_loop(i * half, (i + 1) * half, middle, 0, unroll=5 if half % 5 == 0 else 1)
        for q in range(1, L - 1):
            send_bulk(q, i)

    for c in halos:
        c.wait_recv()

    k_top = staged(jnp.concatenate([halo_k[0], kap_ref[0 : B + HALO]], axis=0), steps)

    def top(g, _):
        v = [
            diffuse(jnp.concatenate([halo_x[0, 2 * g + e], x_ref[2 * g + e, 0 : B + HALO, :]], axis=0), k_top)
            for e in range(2)
        ]
        for e in range(2):
            out_ref[2 * g + e, 0:B, :] = v[e][HALO : HALO + B]
        keep(v, HALO, 0, g, [(0, 0)])
        return 0

    for i in range(parts):
        lax.fori_loop(i * half, (i + 1) * half, top, 0, unroll=5 if half % 5 == 0 else 1)
        send_bulk(0, i)

    k_bot = staged(jnp.concatenate([kap_ref[R - B - HALO : R], halo_k[1]], axis=0), steps)

    def bottom(g, _):
        v = [
            diffuse(
                jnp.concatenate([x_ref[2 * g + e, R - B - HALO : R, :], halo_x[1, 2 * g + e]], axis=0), k_bot
            )
            for e in range(2)
        ]
        for e in range(2):
            out_ref[2 * g + e, R - B : R, :] = v[e][HALO : HALO + B]
        keep(v, HALO, R - B, g, [(L - 1, R - B)])
        return 0

    for i in range(parts):
        lax.fori_loop(i * half, (i + 1) * half, bottom, 0, unroll=5 if half % 5 == 0 else 1)
        send_bulk(L - 1, i)

    for c in loads[3:8]:
        c.wait()
    inv = inv_ref[...]
    first = lax.broadcasted_iota(jnp.int32, (LEV, LEV), 0)
    second = lax.broadcasted_iota(jnp.int32, (LEV, LEV), 1)
    mix = inv - jnp.where(first == second, 1.0, 0.0)
    mix_hi = mix.astype(BF16)
    mix_lo = (mix - mix_hi.astype(F32)).astype(BF16)
    cs[...] = jnp.broadcast_to(jnp.sum(inv * imp_ref[...], axis=1, keepdims=True), (LEV, W))

    for q in range(L):
        lo, at, n = window(q)

        @pl.when(l == q)
        def _(q=q, at=at, n=n):
            for p in range(L):
                remote(
                    p_buf.at[pl.ds(0, n)], part.at[p, pl.ds(at, n)], part_s.at[q], part_r.at[p], (other, h, p)
                ).wait_recv()
            remote(kap_ref.at[pl.ds(0, n)], kapw.at[pl.ds(at, n)], kapw_s, kapw_r, (other, h, q)).wait_recv()
            if q == 0 or q == L - 1:
                at_e = 0 if q == 0 else WIN - MARGIN
                for p in range(L):
                    remote(
                        p_buf.at[pl.ds(0, MARGIN)],
                        part.at[p, pl.ds(at_e, MARGIN)],
                        pedge_s.at[0],
                        pedge_r.at[p],
                        (other, h, p),
                    ).wait_recv()
                remote(
                    kap_ref.at[pl.ds(0, MARGIN)], kapw.at[pl.ds(at_e, MARGIN)], kedge_s, kedge_r, (other, h, q)
                ).wait_recv()

    total = part[0]
    for p in range(1, L):
        total = total + part[p]
    surface = diffuse(total, staged(kapw[...], steps_other)).astype(BF16)

    first_row = (h * L + l) * B
    rows_total = H * L * B
    place = rows_ref[...] - first_row + REACH
    place = jnp.where(place < 0, place + rows_total, place)
    place = jnp.where(place >= rows_total, place - rows_total, place) + HALO
    pairs = place.shape[0]
    counts = counts_ref[...]
    cells = lax.broadcasted_iota(jnp.int32, (WIN, B), 0)
    sources = jnp.concatenate(
        [
            lax.dot_general(
                jnp.where((cells == place[j]) & (counts > j), 1.0, 0.0).astype(BF16),
                surface,
                (((0,), (0,)), ((), ())),
                preferred_element_type=F32,
            ).astype(BF16)
            for j in range(pairs)
        ],
        axis=1,
    )
    loads[8].wait()
    row_of = lax.broadcasted_iota(jnp.int32, (B, W), 0)
    forcing = jnp.zeros((B, W), F32)
    for r in range(B):
        product = jnp.dot(sources, w_buf[r * pairs * W : (r + 1) * pairs * W, :], preferred_element_type=F32)
        forcing = jnp.where(row_of == r, product, forcing)
    f_ref[...] = forcing
    fm[l] = forcing * mask_ref[...].astype(F32)

    def fm_copy(d, slot):
        peer = lax.rem(l + d, L)
        return remote(fm.at[slot], fm.at[slot], fm_s.at[d - 1], fm_r.at[slot], (s, h, peer))

    for d in range(1, L):
        fm_copy(d, l).start()

    for q in range(L):

        @pl.when(l != q)
        def _(q=q):
            for i in range(parts):
                bulk_copy(q, q, i).wait_recv()

    def ret_copy(q, t, slot):
        return remote(y16.at[q, t], yr.at[slot, t], ret_s.at[q, t], ret_r.at[slot, t], (s, h, q))

    for t in range(T):
        for q in range(L):
            c_buf[t, q * K * 8 : (q + 1) * K * 8, :] = col16[q, t].astype(F32).reshape(K * 8, W)
        for r in range(0, 8, 2):
            x = jnp.concatenate(
                [c_buf[t, pl.ds(r + e, LEV, stride=8), :] for e in range(2)], axis=1
            ).astype(BF16)
            y = jnp.dot(mix_hi, x, preferred_element_type=F32) + jnp.dot(
                mix_lo, x, preferred_element_type=F32
            )
            for e in range(2):
                z_buf[t, pl.ds(r + e, LEV, stride=8), :] = y[:, e * W : (e + 1) * W]
        for q in range(L):
            y16[q, t] = z_buf[t, q * K * 8 : (q + 1) * K * 8, :].reshape(G, 16, W).astype(BF16)
        for q in range(L):

            @pl.when(l != q)
            def _(q=q, t=t):
                ret_copy(q, t, l).start()

            @pl.when(l == q)
            def _(q=q, t=t):
                yr[q, t] = y16[q, t]

    for d in range(1, L):
        fm_copy(d, lax.rem(l + d, L)).wait_recv()

    for t in range(T):
        for q in range(L):

            @pl.when(l != q)
            def _(q=q, t=t):
                ret_copy(q, t, q).wait_recv()

        def finish(g, _, t=t):
            for e in range(2):
                k = 2 * g + e
                c = cs[pl.ds(l * K + k, 1), :]
                for q in range(L):
                    at = q * B + 8 * t
                    y = yr[q, t, g].astype(F32)[8 * e : 8 * e + 8]
                    out_ref[k, at : at + 8, :] = out_ref[k, at : at + 8, :] + (
                        y + c * fm[q, 8 * t : 8 * t + 8, :]
                    )
            return 0

        lax.fori_loop(0, G, finish, 0, unroll=5 if G % 5 == 0 else 1)

    for c in halos:
        c.wait_send()
    for q in range(L):
        part_copy(q).wait_send()

        @pl.when(l == q)
        def _(q=q):
            kap_copy(q).wait_send()

        @pl.when(l != q)
        def _(q=q):
            for i in range(parts):
                bulk_copy(q, l, i).wait_send()
            for t in range(T):
                ret_copy(q, t, l).wait_send()

    edge_low.wait_send()
    edge_high.wait_send()

    @pl.when(l == 0)
    def _():
        kedge_low.wait_send()

    @pl.when(l == L - 1)
    def _():
        kedge_high.wait_send()

    for d in range(1, L):
        fm_copy(d, l).wait_send()


def per_device(
    state,
    diffusivity,
    coupling_mask,
    pair_rows,
    pair_counts,
    remap_weights,
    export_profile,
    import_profile,
    column_inverse,
):
    _, K, R, W = state.shape
    H = lax.axis_size("horiz")
    L = lax.axis_size("lev")
    B = R // L
    T = B // 8
    G = K // 2
    WIN = B + 2 * MARGIN
    LEV = K * L
    pairs = pair_rows.shape[2]
    weights = remap_weights.reshape(B * pairs * W, W)
    vmem = pl.BlockSpec(memory_space=pltpu.VMEM)
    hbm = pl.BlockSpec(memory_space=pltpu.HBM)
    dma = pltpu.SemaphoreType.DMA
    new_state, forcing = pl.pallas_call(
        functools.partial(kernel, (H, L, K, R, W)),
        out_shape=(pltpu.VMEM((K, R, W), F32), pltpu.VMEM((B, W), F32)),
        in_specs=[hbm] * 9,
        out_specs=(vmem, vmem),
        scratch_shapes=[
            pltpu.VMEM((K, R, W), F32),
            pltpu.VMEM((R, W), F32),
            pltpu.VMEM((B, W), jnp.int32),
            pltpu.VMEM((pairs, 1, B), jnp.int32),
            pltpu.VMEM((1, B), jnp.int32),
            pltpu.VMEM(weights.shape, BF16),
            pltpu.SMEM((1, LEV), F32),
            pltpu.VMEM((1, LEV), F32),
            pltpu.VMEM((LEV, LEV), F32),
            pltpu.VMEM((R, W), F32),
            pltpu.VMEM((L, WIN, W), F32),
            pltpu.VMEM((WIN, W), F32),
            pltpu.VMEM((2, K, HALO, W), F32),
            pltpu.VMEM((2, HALO, W), F32),
            pltpu.VMEM((L, T, G, 16, W), BF16),
            pltpu.VMEM((L, T, G, 16, W), BF16),
            pltpu.VMEM((T, LEV * 8, W), F32),
            pltpu.VMEM((T, LEV * 8, W), F32),
            pltpu.VMEM((L, T, G, 16, W), BF16),
            pltpu.VMEM((L, T, G, 16, W), BF16),
            pltpu.VMEM((L, B, W), F32),
            pltpu.VMEM((LEV, W), F32),
            dma((9,)),
            dma((2,)),
            dma((2,)),
            dma((2,)),
            dma((2,)),
            dma((L,)),
            dma((L,)),
            dma((2,)),
            dma((L,)),
            dma,
            dma,
            dma,
            dma,
            dma((L, 2)),
            dma((L, 2)),
            dma((L - 1,)),
            dma((L,)),
            dma((L, T)),
            dma((L, T)),
        ],
        compiler_params=pltpu.CompilerParams(
            collective_id=0, has_side_effects=True, vmem_limit_bytes=56 * 1024 * 1024
        ),
    )(
        state[0],
        diffusivity[0],
        coupling_mask[0],
        jnp.transpose(pair_rows, (2, 0, 1)),
        pair_counts,
        weights,
        export_profile,
        import_profile,
        column_inverse[0],
    )
    return (new_state[None], forcing[None])


def solution(mesh):
    placed = (
        P("sec", "lev", "horiz", None),
        P("sec", "horiz", None),
        P("sec", ("horiz", "lev"), None),
        P("sec", ("horiz", "lev"), None),
        P("sec", ("horiz", "lev")),
        P("sec", ("horiz", "lev"), None, None, None),
        P("sec", None),
        P("sec", None),
        P("sec", None, None),
    )
    return jax.shard_map(
        per_device,
        mesh=mesh,
        in_specs=placed,
        out_specs=(P("sec", "lev", "horiz", None), P("sec", ("horiz", "lev"), None)),
        check_vma=False,
    )
```

```python
import functools

import jax
import jax.numpy as jnp
from jax import lax
from jax.experimental import pallas as pl
from jax.experimental.pallas import tpu as pltpu
from jax.sharding import PartitionSpec as P

REACH = 8
ATM_STEPS = 4
OCN_STEPS = 2
HALO = 8
MARGIN = REACH + HALO
F32 = jnp.float32
BF16 = jnp.bfloat16


def diffuse(v, kappas):
    rows = v.shape[0]
    for k in kappas:
        around = (
            pltpu.roll(v, 1, 0)
            + pltpu.roll(v, rows - 1, 0)
            + pltpu.roll(v, 1, 1)
            + pltpu.roll(v, v.shape[1] - 1, 1)
        )
        v = v + k * (around - 4.0 * v)
    return v


def kernel(
    sizes,
    x_hbm,
    kap_hbm,
    mask_hbm,
    rows_hbm,
    counts_hbm,
    w_hbm,
    exp_hbm,
    imp_hbm,
    inv_hbm,
    out_ref,
    f_ref,
    x_ref,
    kap_ref,
    mask_ref,
    rows_ref,
    counts_ref,
    w_buf,
    exp_ref,
    imp_ref,
    inv_ref,
    p_buf,
    part,
    kapw,
    halo_x,
    halo_k,
    dyn16,
    col16,
    c_buf,
    z_buf,
    y16,
    yr,
    fm,
    cs,
    in_sem,
    halo_s,
    halo_r,
    halok_s,
    halok_r,
    part_s,
    part_r,
    pedge_s,
    pedge_r,
    kapw_s,
    kapw_r,
    kedge_s,
    kedge_r,
    bulk_s,
    bulk_r,
    fm_s,
    fm_r,
    ret_s,
    ret_r,
):
    H, L, K, R, W = sizes
    B = R // L
    T = B // 8
    G = K // 2
    WIN = B + 2 * MARGIN
    LEV = K * L
    s = lax.axis_index("sec")
    h = lax.axis_index("horiz")
    l = lax.axis_index("lev")
    other = 1 - s
    nxt = lax.rem(h + 1, H)
    prv = lax.rem(h + H - 1, H)

    def remote(src, dst, ssem, rsem, dev):
        return pltpu.make_async_remote_copy(
            src_ref=src,
            dst_ref=dst,
            send_sem=ssem,
            recv_sem=rsem,
            device_id=dev,
            device_id_type=pl.DeviceIdType.MESH,
        )

    loads = [
        pltpu.make_async_copy(src, dst, in_sem.at[i])
        for i, (src, dst) in enumerate(
            (
                (x_hbm, x_ref),
                (exp_hbm, exp_ref),
                (kap_hbm, kap_ref),
                (inv_hbm, inv_ref),
                (imp_hbm, imp_ref),
                (rows_hbm, rows_ref),
                (counts_hbm, counts_ref),
                (mask_hbm, mask_ref),
                (w_hbm, w_buf),
            )
        )
    ]
    for c in loads:
        c.start()

    barrier = pltpu.get_barrier_semaphore()

    def greet(dev):
        pl.semaphore_signal(barrier, inc=1, device_id=dev, device_id_type=pl.DeviceIdType.MESH)

    for d in range(1, L):
        greet((s, h, lax.rem(l + d, L)))
    greet((s, nxt, l))
    greet((s, prv, l))
    for q in range(L):
        greet((other, h, q))

    @pl.when(l == 0)
    def _():
        for q in range(L):
            greet((other, prv, q))

    @pl.when(l == L - 1)
    def _():
        for q in range(L):
            greet((other, nxt, q))

    loads[0].wait()
    loads[1].wait()

    def add_level(k, acc):
        return acc + exp_ref[0, l * K + k] * x_ref[k]

    loads[2].wait()
    pl.semaphore_wait(barrier, (L - 1) + 2 + L + 2)

    halos = [
        remote(x_ref.at[:, pl.ds(R - HALO, HALO)], halo_x.at[0], halo_s.at[0], halo_r.at[0], (s, nxt, l)),
        remote(x_ref.at[:, pl.ds(0, HALO)], halo_x.at[1], halo_s.at[1], halo_r.at[1], (s, prv, l)),
        remote(kap_ref.at[pl.ds(R - HALO, HALO)], halo_k.at[0], halok_s.at[0], halok_r.at[0], (s, nxt, l)),
        remote(kap_ref.at[pl.ds(0, HALO)], halo_k.at[1], halok_s.at[1], halok_r.at[1], (s, prv, l)),
    ]
    for c in halos:
        c.start()

    p_buf[...] = lax.fori_loop(0, K, add_level, jnp.zeros((R, W), F32), unroll=4)

    def window(q):
        lo = max(q * B - MARGIN, 0)
        hi = min(q * B + B + MARGIN, R)
        return lo, lo - (q * B - MARGIN), hi - lo

    def part_copy(q):
        lo, at, n = window(q)
        return remote(
            p_buf.at[pl.ds(lo, n)], part.at[l, pl.ds(at, n)], part_s.at[q], part_r.at[l], (other, h, q)
        )

    def kap_copy(q):
        lo, at, n = window(q)
        return remote(kap_ref.at[pl.ds(lo, n)], kapw.at[pl.ds(at, n)], kapw_s, kapw_r, (other, h, q))

    edge_low = remote(
        p_buf.at[pl.ds(R - MARGIN, MARGIN)],
        part.at[l, pl.ds(0, MARGIN)],
        pedge_s.at[0],
        pedge_r.at[l],
        (other, nxt, 0),
    )
    edge_high = remote(
        p_buf.at[pl.ds(0, MARGIN)],
        part.at[l, pl.ds(WIN - MARGIN, MARGIN)],
        pedge_s.at[1],
        pedge_r.at[l],
        (other, prv, L - 1),
    )
    kedge_low = remote(
        kap_ref.at[pl.ds(R - MARGIN, MARGIN)], kapw.at[pl.ds(0, MARGIN)], kedge_s, kedge_r, (other, nxt, 0)
    )
    kedge_high = remote(
        kap_ref.at[pl.ds(0, MARGIN)],
        kapw.at[pl.ds(WIN - MARGIN, MARGIN)],
        kedge_s,
        kedge_r,
        (other, prv, L - 1),
    )
    for q in range(L):
        part_copy(q).start()
    edge_low.start()
    edge_high.start()
    for q in range(L):

        @pl.when(l == q)
        def _(q=q):
            kap_copy(q).start()

    @pl.when(l == 0)
    def _():
        kedge_low.start()

    @pl.when(l == L - 1)
    def _():
        kedge_high.start()

    steps = jnp.where(s == 0, ATM_STEPS, OCN_STEPS)
    steps_other = jnp.where(s == 0, OCN_STEPS, ATM_STEPS)

    def staged(k, count):
        return [k if i < OCN_STEPS else jnp.where(i < count, k, 0.0) for i in range(ATM_STEPS)]

    def keep(v, at, first, g, levels):
        for q, row in levels:
            for t in range(T):
                lo = row + 8 * t - first + at
                dyn16[q, t, g] = jnp.concatenate([v[0][lo : lo + 8], v[1][lo : lo + 8]], axis=0).astype(BF16)

    half = G // 2 if G % 2 == 0 else G
    parts = G // half

    def bulk_copy(q, dst_slot, i):
        piece = pl.ds(i * half, half)
        return remote(
            dyn16.at[q, :, piece],
            col16.at[dst_slot, :, piece],
            bulk_s.at[q, i],
            bulk_r.at[dst_slot, i],
            (s, h, q),
        )

    def send_bulk(q, i):
        @pl.when(l != q)
        def _():
            bulk_copy(q, l, i).start()

        @pl.when(l == q)
        def _():
            piece = pl.ds(i * half, half)
            col16[q, :, piece] = dyn16[q, :, piece]

    lo_c, hi_c = B - HALO, R - B + HALO
    k_mid = staged(kap_ref[lo_c:hi_c], steps)

    def middle(g, _):
        v = [diffuse(x_ref[2 * g + e, lo_c:hi_c, :], k_mid) for e in range(2)]
        for e in range(2):
            out_ref[2 * g + e, B : R - B, :] = v[e][HALO : HALO + R - 2 * B]
        keep(v, 0, lo_c, g, [(q, q * B) for q in range(1, L - 1)])
        return 0

    for i in range(parts):
        lax.fori_loop(i * half, (i + 1) * half, middle, 0, unroll=5 if half % 5 == 0 else 1)
        for q in range(1, L - 1):
            send_bulk(q, i)

    for c in halos:
        c.wait_recv()

    k_top = staged(jnp.concatenate([halo_k[0], kap_ref[0 : B + HALO]], axis=0), steps)

    def top(g, _):
        v = [
            diffuse(jnp.concatenate([halo_x[0, 2 * g + e], x_ref[2 * g + e, 0 : B + HALO, :]], axis=0), k_top)
            for e in range(2)
        ]
        for e in range(2):
            out_ref[2 * g + e, 0:B, :] = v[e][HALO : HALO + B]
        keep(v, HALO, 0, g, [(0, 0)])
        return 0

    for i in range(parts):
        lax.fori_loop(i * half, (i + 1) * half, top, 0, unroll=5 if half % 5 == 0 else 1)
        send_bulk(0, i)

    k_bot = staged(jnp.concatenate([kap_ref[R - B - HALO : R], halo_k[1]], axis=0), steps)

    def bottom(g, _):
        v = [
            diffuse(
                jnp.concatenate([x_ref[2 * g + e, R - B - HALO : R, :], halo_x[1, 2 * g + e]], axis=0), k_bot
            )
            for e in range(2)
        ]
        for e in range(2):
            out_ref[2 * g + e, R - B : R, :] = v[e][HALO : HALO + B]
        keep(v, HALO, R - B, g, [(L - 1, R - B)])
        return 0

    for i in range(parts):
        lax.fori_loop(i * half, (i + 1) * half, bottom, 0, unroll=5 if half % 5 == 0 else 1)
        send_bulk(L - 1, i)

    for c in loads[3:8]:
        c.wait()
    inv = inv_ref[...]
    first = lax.broadcasted_iota(jnp.int32, (LEV, LEV), 0)
    second = lax.broadcasted_iota(jnp.int32, (LEV, LEV), 1)
    mix = inv - jnp.where(first == second, 1.0, 0.0)
    mix_hi = mix.astype(BF16)
    mix_lo = (mix - mix_hi.astype(F32)).astype(BF16)
    cs[...] = jnp.broadcast_to(jnp.sum(inv * imp_ref[...], axis=1, keepdims=True), (LEV, W))

    for q in range(L):
        lo, at, n = window(q)

        @pl.when(l == q)
        def _(q=q, at=at, n=n):
            for p in range(L):
                remote(
                    p_buf.at[pl.ds(0, n)], part.at[p, pl.ds(at, n)], part_s.at[q], part_r.at[p], (other, h, p)
                ).wait_recv()
            remote(kap_ref.at[pl.ds(0, n)], kapw.at[pl.ds(at, n)], kapw_s, kapw_r, (other, h, q)).wait_recv()
            if q == 0 or q == L - 1:
                at_e = 0 if q == 0 else WIN - MARGIN
                for p in range(L):
                    remote(
                        p_buf.at[pl.ds(0, MARGIN)],
                        part.at[p, pl.ds(at_e, MARGIN)],
                        pedge_s.at[0],
                        pedge_r.at[p],
                        (other, h, p),
                    ).wait_recv()
                remote(
                    kap_ref.at[pl.ds(0, MARGIN)], kapw.at[pl.ds(at_e, MARGIN)], kedge_s, kedge_r, (other, h, q)
                ).wait_recv()

    total = part[0]
    for p in range(1, L):
        total = total + part[p]
    surface = diffuse(total, staged(kapw[...], steps_other)).astype(BF16)

    first_row = (h * L + l) * B
    rows_total = H * L * B
    place = rows_ref[...] - first_row + REACH
    place = jnp.where(place < 0, place + rows_total, place)
    place = jnp.where(place >= rows_total, place - rows_total, place) + HALO
    pairs = place.shape[0]
    counts = counts_ref[...]
    cells = lax.broadcasted_iota(jnp.int32, (WIN, B), 0)
    sources = jnp.concatenate(
        [
            lax.dot_general(
                jnp.where((cells == place[j]) & (counts > j), 1.0, 0.0).astype(BF16),
                surface,
                (((0,), (0,)), ((), ())),
                preferred_element_type=F32,
            ).astype(BF16)
            for j in range(pairs)
        ],
        axis=1,
    )
    loads[8].wait()
    row_of = lax.broadcasted_iota(jnp.int32, (B, W), 0)
    forcing = jnp.zeros((B, W), F32)
    for r in range(B):
        product = jnp.dot(sources, w_buf[r * pairs * W : (r + 1) * pairs * W, :], preferred_element_type=F32)
        forcing = jnp.where(row_of == r, product, forcing)
    f_ref[...] = forcing
    fm[l] = forcing * mask_ref[...].astype(F32)

    def fm_copy(d, slot):
        peer = lax.rem(l + d, L)
        return remote(fm.at[slot], fm.at[slot], fm_s.at[d - 1], fm_r.at[slot], (s, h, peer))

    for d in range(1, L):
        fm_copy(d, l).start()

    for q in range(L):

        @pl.when(l != q)
        def _(q=q):
            for i in range(parts):
                bulk_copy(q, q, i).wait_recv()

    def ret_copy(q, t, slot):
        return remote(y16.at[q, t], yr.at[slot, t], ret_s.at[q, t], ret_r.at[slot, t], (s, h, q))

    for t in range(T):
        for q in range(L):
            c_buf[t, q * K * 8 : (q + 1) * K * 8, :] = col16[q, t].astype(F32).reshape(K * 8, W)
        for r in range(0, 8, 2):
            x = jnp.concatenate(
                [c_buf[t, pl.ds(r + e, LEV, stride=8), :] for e in range(2)], axis=1
            ).astype(BF16)
            y = jnp.dot(mix_hi, x, preferred_element_type=F32) + jnp.dot(
                mix_lo, x, preferred_element_type=F32
            )
            for e in range(2):
                z_buf[t, pl.ds(r + e, LEV, stride=8), :] = y[:, e * W : (e + 1) * W]
        for q in range(L):
            y16[q, t] = z_buf[t, q * K * 8 : (q + 1) * K * 8, :].reshape(G, 16, W).astype(BF16)
        for q in range(L):

            @pl.when(l != q)
            def _(q=q, t=t):
                ret_copy(q, t, l).start()

            @pl.when(l == q)
            def _(q=q, t=t):
                yr[q, t] = y16[q, t]

    for d in range(1, L):
        fm_copy(d, lax.rem(l + d, L)).wait_recv()

    for t in range(T):
        for q in range(L):

            @pl.when(l != q)
            def _(q=q, t=t):
                ret_copy(q, t, q).wait_recv()

        def finish(g, _, t=t):
            for e in range(2):
                k = 2 * g + e
                c = cs[pl.ds(l * K + k, 1), :]
                for q in range(L):
                    at = q * B + 8 * t
                    y = yr[q, t, g].astype(F32)[8 * e : 8 * e + 8]
                    out_ref[k, at : at + 8, :] = out_ref[k, at : at + 8, :] + (
                        y + c * fm[q, 8 * t : 8 * t + 8, :]
                    )
            return 0

        lax.fori_loop(0, G, finish, 0, unroll=5 if G % 5 == 0 else 1)

    for c in halos:
        c.wait_send()
    for q in range(L):
        part_copy(q).wait_send()

        @pl.when(l == q)
        def _(q=q):
            kap_copy(q).wait_send()

        @pl.when(l != q)
        def _(q=q):
            for i in range(parts):
                bulk_copy(q, l, i).wait_send()
            for t in range(T):
                ret_copy(q, t, l).wait_send()

    edge_low.wait_send()
    edge_high.wait_send()

    @pl.when(l == 0)
    def _():
        kedge_low.wait_send()

    @pl.when(l == L - 1)
    def _():
        kedge_high.wait_send()

    for d in range(1, L):
        fm_copy(d, l).wait_send()


def per_device(
    state,
    diffusivity,
    coupling_mask,
    pair_rows,
    pair_counts,
    remap_weights,
    export_profile,
    import_profile,
    column_inverse,
):
    _, K, R, W = state.shape
    H = lax.axis_size("horiz")
    L = lax.axis_size("lev")
    B = R // L
    T = B // 8
    G = K // 2
    WIN = B + 2 * MARGIN
    LEV = K * L
    pairs = pair_rows.shape[2]
    weights = remap_weights.reshape(B * pairs * W, W)
    vmem = pl.BlockSpec(memory_space=pltpu.VMEM)
    hbm = pl.BlockSpec(memory_space=pltpu.HBM)
    dma = pltpu.SemaphoreType.DMA
    new_state, forcing = pl.pallas_call(
        functools.partial(kernel, (H, L, K, R, W)),
        out_shape=(pltpu.VMEM((K, R, W), F32), pltpu.VMEM((B, W), F32)),
        in_specs=[hbm] * 9,
        out_specs=(vmem, vmem),
        scratch_shapes=[
            pltpu.VMEM((K, R, W), F32),
            pltpu.VMEM((R, W), F32),
            pltpu.VMEM((B, W), jnp.int32),
            pltpu.VMEM((pairs, 1, B), jnp.int32),
            pltpu.VMEM((1, B), jnp.int32),
            pltpu.VMEM(weights.shape, BF16),
            pltpu.SMEM((1, LEV), F32),
            pltpu.VMEM((1, LEV), F32),
            pltpu.VMEM((LEV, LEV), F32),
            pltpu.VMEM((R, W), F32),
            pltpu.VMEM((L, WIN, W), F32),
            pltpu.VMEM((WIN, W), F32),
            pltpu.VMEM((2, K, HALO, W), F32),
            pltpu.VMEM((2, HALO, W), F32),
            pltpu.VMEM((L, T, G, 16, W), BF16),
            pltpu.VMEM((L, T, G, 16, W), BF16),
            pltpu.VMEM((T, LEV * 8, W), F32),
            pltpu.VMEM((T, LEV * 8, W), F32),
            pltpu.VMEM((L, T, G, 16, W), BF16),
            pltpu.VMEM((L, T, G, 16, W), BF16),
            pltpu.VMEM((L, B, W), F32),
            pltpu.VMEM((LEV, W), F32),
            dma((9,)),
            dma((2,)),
            dma((2,)),
            dma((2,)),
            dma((2,)),
            dma((L,)),
            dma((L,)),
            dma((2,)),
            dma((L,)),
            dma,
            dma,
            dma,
            dma,
            dma((L, 2)),
            dma((L, 2)),
            dma((L - 1,)),
            dma((L,)),
            dma((L, T)),
            dma((L, T)),
        ],
        compiler_params=pltpu.CompilerParams(
            collective_id=0, has_side_effects=True, vmem_limit_bytes=56 * 1024 * 1024
        ),
    )(
        state[0],
        diffusivity[0],
        coupling_mask[0],
        jnp.transpose(pair_rows, (2, 0, 1)),
        pair_counts,
        weights,
        export_profile,
        import_profile,
        column_inverse[0],
    )
    return (new_state[None], forcing[None])


def solution(mesh):
    placed = (
        P("sec", "lev", "horiz", None),
        P("sec", "horiz", None),
        P("sec", ("horiz", "lev"), None),
        P("sec", ("horiz", "lev"), None),
        P("sec", ("horiz", "lev")),
        P("sec", ("horiz", "lev"), None, None, None),
        P("sec", None),
        P("sec", None),
        P("sec", None, None),
    )
    return jax.shard_map(
        per_device,
        mesh=mesh,
        in_specs=placed,
        out_specs=(P("sec", "lev", "horiz", None), P("sec", ("horiz", "lev"), None)),
        check_vma=False,
    )
```
